1024 devices in a mesh: group: 16 (over y, core), expert: 64 (over z, x).
Axes of the slice: x: 4, y: 8, z: 16, core: 2. Of those that a mesh axis runs over, the one named last changes fastest.
Arguments:
- x_rows: bfloat16 [16, 64, 1, 7168], P('group', 'expert'), may hold values from -6 to 6
- grad_rows: bfloat16 [16, 64, 1, 7168], P('group', 'expert'), may hold values from -6 to 6
- routes: int32 [16, 64, 1, 8], replicated, may hold values from 0 to 63, as said below
- probs: bfloat16 [16, 64, 1, 8], replicated, may hold values from 0.099609375 to 1
- w_gate: bfloat16 [1024, 448, 1024], P(('group', 'expert')), may hold values from -0.0625 to 0.0625
- w_up: bfloat16 [1024, 448, 1024], P(('group', 'expert')), may hold values from -0.0625 to 0.0625
- w_down: bfloat16 [1024, 1024, 448], P(('group', 'expert')), may hold values from -0.1875 to 0.1875
Outputs:
- grad_input: bfloat16 [16, 64, 1, 7168], P('group', 'expert')
The draws below stay inside these ranges and needn't reach their ends.
Inputs may be any that keep to these rules, and one draw needn't show every extreme that they name: `routes`: each token names 8 different experts from exactly 4 different groups (group of expert j: j // 4), at least one expert in each of them. In each column every group is used by exactly 4 of its 16 tokens, so no expert is named more than 4 times in a column; in every draw some expert is named exactly 4 times in some column.
All inputs are finite; a program needn't handle non-finite values.
Results may differ from the reference program's by a relative error of at most 0.023.
Values may be sent and summed in bfloat16 or wider, within the bound.
A program may use at most 32 MiB of HBM per device.

```python
import jax
import jax.numpy as jnp
from jax import lax

D = 7168
FF = 1024
TOPK = 8
TOPG = 4
EPG = 4
TOK_DEV = 1
EXPERTS = 64
PIECES = 16
COLTOK = 16
CAPE = 4
N_GROUP = 16
N_EXPERT = 64


def draw_routes(key, part):
    key = jax.random.fold_in(key, 7)
    subkeys = jax.random.split(key, 6)
    columns = N_EXPERT
    tokens = COLTOK
    spare_slots = TOPG * (EPG - 1)
    extra_count = TOPK - TOPG
    group_order = jax.vmap(lambda subkey: jax.random.permutation(subkey, N_GROUP))(jax.random.split(subkeys[0], columns))
    offsets = jax.vmap(lambda subkey: jax.random.permutation(subkey, N_GROUP)[:TOPG])(jax.random.split(subkeys[1], columns))
    positions = jnp.arange(tokens, dtype=jnp.int32)
    residues = (positions[None, :, None] + offsets[:, None, :]) % N_GROUP
    chosen_groups = jax.vmap(lambda lookup, where_at: lookup[where_at])(group_order, residues)
    spare_ids = jnp.arange(spare_slots, dtype=jnp.int32)
    spare_scores = jax.random.randint(subkeys[2], (columns, tokens, spare_slots), 0, 1 << 20) * spare_slots + spare_ids
    spare_rank = jnp.sum(spare_scores[..., None, :] > spare_scores[..., :, None], axis=-1)
    taken_slots = (spare_rank < extra_count).astype(jnp.int32)
    owner_group = spare_ids // (EPG - 1)
    group_slots = jnp.arange(TOPG, dtype=jnp.int32)
    counts = 1 + jnp.sum(taken_slots[:, :, None, :] * (owner_group[None, None, None, :] == group_slots[None, None, :, None]).astype(jnp.int32), axis=-1)
    popular = jax.random.randint(subkeys[3], (N_GROUP, EPG), 0, 4) * 16
    noise_terms = jax.random.randint(subkeys[4], (columns, tokens, TOPG, EPG), 0, 16)
    favored = jax.random.randint(subkeys[5], (N_GROUP,), 0, EPG)
    local_ids = jnp.arange(EPG, dtype=jnp.int32)
    favor_table = (local_ids[None, :] == favored[:, None]).astype(jnp.int32)
    first_column = (jnp.arange(columns, dtype=jnp.int32) == 0).astype(jnp.int32)[:, None, None, None]
    expert_score = (popular[chosen_groups] + noise_terms + 1000 * favor_table[chosen_groups] * first_column) * EPG + local_ids
    expert_rank = jnp.sum(expert_score[..., None, :] > expert_score[..., :, None], axis=-1)
    picked = expert_rank < counts[..., None]
    expert_ids = chosen_groups[..., None] * EPG + local_ids
    order_keys = jnp.where(picked, expert_ids, expert_ids + EXPERTS).reshape(columns, tokens, TOPG * EPG)
    routes_cols = jnp.sort(order_keys, axis=-1)[..., :TOPK]
    return jnp.transpose(routes_cols.reshape(columns, N_GROUP, TOK_DEV, TOPK), (1, 0, 2, 3)).astype(jnp.int32)


def levels(key, dims, shards, low, top_value):
    level, own = 1.0, jax.random.fold_in(key, 6)
    for axis_at, blocks in shards:
        draws = jnp.exp(jax.random.uniform(jax.random.fold_in(own, axis_at), (blocks,), jnp.float32, low / len(shards), top_value / len(shards)))
        level = level * jnp.repeat(draws, dims[axis_at] // blocks).reshape([-1 if axis == axis_at else 1 for axis in range(len(dims))])
    return level


def centred(rng, extent, width, reach, cuts=(), held_as=jnp.bfloat16):
    values = width * jax.random.normal(rng, extent, jnp.float32)
    if cuts:
        values = values * levels(rng, extent, cuts, -0.22, 0.18)
    return jnp.clip(values, -reach, reach).astype(held_as)


def setup_inputs(seed: int = 0) -> dict:
    arg_keys = jax.random.split(jax.random.key(seed), 8)
    return {
        "x_rows": centred(arg_keys[0], (N_GROUP, N_EXPERT, TOK_DEV, D), 1.0, 6.0, ((0, 16), (1, 64))),
        "grad_rows": centred(arg_keys[1], (N_GROUP, N_EXPERT, TOK_DEV, D), 1.0, 6.0, ((0, 16), (1, 64))),
        "routes": draw_routes(jax.random.fold_in(arg_keys[7], 71), 0),
        "probs": jnp.clip(jax.random.uniform(arg_keys[3], (N_GROUP, N_EXPERT, TOK_DEV, TOPK), jnp.float32, 0.099609375, 1.0), 0.099609375, 1.0).astype(jnp.bfloat16),
        "w_gate": centred(arg_keys[4], (EXPERTS * PIECES, D // PIECES, FF), D ** -0.5, 0.0625, ((0, 1024),)),
        "w_up": centred(arg_keys[5], (EXPERTS * PIECES, D // PIECES, FF), D ** -0.5, 0.0625, ((0, 1024),)),
        "w_down": centred(arg_keys[6], (EXPERTS * PIECES, FF, D // PIECES), FF ** -0.5, 0.1875, ((0, 1024),)),
    }


def reference(x_rows, grad_rows, routes, probs, w_gate, w_up, w_down):
    highest = lax.Precision.HIGHEST
    x_wide = jnp.transpose(x_rows, (1, 0, 2, 3)).reshape(N_EXPERT, COLTOK, D).astype(jnp.float32)
    g_wide = jnp.transpose(grad_rows, (1, 0, 2, 3)).reshape(N_EXPERT, COLTOK, D).astype(jnp.float32)
    route_cols = jnp.transpose(routes, (1, 0, 2, 3)).reshape(N_EXPERT, COLTOK, TOPK)
    prob_cols = jnp.transpose(probs, (1, 0, 2, 3)).reshape(N_EXPERT, COLTOK, TOPK).astype(jnp.float32)
    gate_full = w_gate.reshape(EXPERTS, D, FF)
    up_full = w_up.reshape(EXPERTS, D, FF)
    down_parts = w_down.reshape(EXPERTS, PIECES, FF, D // PIECES)
    expert_ids = jnp.arange(EXPERTS, dtype=jnp.int32)
    slot_ids = jnp.arange(CAPE, dtype=jnp.int32)
    slot_count = N_EXPERT * CAPE

    def expert_step(accumulated, inputs):
        expert, gate_w, up_w, down_w = inputs
        route_hits = route_cols == expert
        named_rows = jnp.any(route_hits, axis=2).astype(jnp.int32)
        earlier = (jnp.cumsum(named_rows, axis=1).astype(jnp.int32) - named_rows).astype(jnp.int32)
        weight = jnp.sum(prob_cols * route_hits.astype(jnp.float32), axis=2)
        mapping = ((named_rows[:, None, :] == 1) & (earlier[:, None, :] == slot_ids[None, :, None])).astype(jnp.float32)
        rows_x = jnp.einsum('csm,cmd->csd', mapping, x_wide, precision=highest).reshape(slot_count, D).astype(jnp.bfloat16)
        rows_g = jnp.einsum('csm,cmd->csd', mapping, g_wide, precision=highest).reshape(slot_count, D).astype(jnp.bfloat16)
        row_p = jnp.sum(mapping * weight[:, None, :], axis=2).reshape(slot_count)
        gate_pre = jnp.dot(rows_x, gate_w, preferred_element_type=jnp.float32)
        up_pre = jnp.dot(rows_x, up_w, preferred_element_type=jnp.float32)
        back_grad = lax.dot_general(rows_g.reshape(slot_count, PIECES, D // PIECES), down_w, (((1, 2), (0, 2)), ((), ())), preferred_element_type=jnp.float32) * row_p[:, None]
        sigmoid_gate = jax.nn.sigmoid(gate_pre)
        grad_gate = (back_grad * up_pre * sigmoid_gate * (1.0 + gate_pre * (1.0 - sigmoid_gate))).astype(jnp.bfloat16)
        grad_up = (back_grad * gate_pre * sigmoid_gate).astype(jnp.bfloat16)
        slot_grad = lax.dot_general(grad_gate, gate_w, (((1,), (1,)), ((), ())), preferred_element_type=jnp.float32) + lax.dot_general(grad_up, up_w, (((1,), (1,)), ((), ())), preferred_element_type=jnp.float32)
        accumulated = accumulated + jnp.einsum('csm,csd->cmd', mapping, slot_grad.reshape(N_EXPERT, CAPE, D), precision=highest)
        return accumulated, None

    accumulated, unused = lax.scan(expert_step, jnp.zeros((N_EXPERT, COLTOK, D), jnp.float32), (expert_ids, gate_full, up_full, down_parts))
    return jnp.transpose(accumulated.reshape(N_EXPERT, N_GROUP, TOK_DEV, D), (1, 0, 2, 3)).astype(jnp.bfloat16)
```

```python
import functools

import jax
import jax.numpy as jnp
from jax import lax
from jax.experimental import pallas as pl
from jax.experimental.pallas import tpu as pltpu
from jax.sharding import PartitionSpec as P

MESH = pl.DeviceIdType.MESH
BLOCKS = 4
RANKS = 4
RING = 4
SLOTS = 4


def low(value, size):
    return value & (size - 1)


def high(value, size):
    return value >> (size.bit_length() - 1)


def onehot(mask):
    return jnp.where(mask, 1.0, 0.0).astype(jnp.bfloat16)


def exact_dot(left, right):
    return jnp.dot(left, right, preferred_element_type=jnp.float32)


def dot_nt(left, right):
    return lax.dot_general(left, right, (((1,), (1,)), ((), ())), preferred_element_type=jnp.float32)


def kernel(
    sizes,
    slot_ref,
    tok_ref,
    rowp_ref,
    wg_hbm,
    wu_hbm,
    wd_hbm,
    out_ref,
    wg,
    wu,
    wd,
    got_a,
    sel,
    got_x,
    blk,
    rows,
    part,
    got_rx,
    part_z,
    got_rz,
    grads,
    ret,
    got_ret,
    ret_x,
    got_retx,
    scat,
    fin,
    w_sem,
    a_send,
    a_recv,
    x_send,
    x_recv,
    z_send,
    z_recv,
    rx_send,
    rx_recv,
    rz_send,
    rz_recv,
    gz_send,
    gz_recv,
    gx_send,
    gx_recv,
    tz_send,
    tz_recv,
    tx_send,
    tx_recv,
    tg_send,
    tg_recv,
):
    groups, blocks, ranks, ring, slots = sizes
    depth = blocks * ranks
    pieces = ranks * ring
    chunk = ring * slots
    width = tok_ref.shape[2]
    hidden = wg.shape[1]
    my_g = lax.axis_index("group")
    my_e = lax.axis_index("expert")
    my_x = low(my_e, ring)
    my_z = high(my_e, ring)
    my_r = low(my_z, ranks)
    z_base = my_z - my_r

    def at_x(x):
        return (my_g, my_z * ring + x)

    def at_z(z):
        return (my_g, z * ring + my_x)

    def at_g(g):
        return (g, my_e)

    def remote(src, dst, send, recv, device):
        return pltpu.make_async_remote_copy(
            src_ref=src, dst_ref=dst, send_sem=send, recv_sem=recv, device_id=device, device_id_type=MESH
        )

    sent = []

    def go(copy):
        copy.start()
        sent.append(copy)

    weight_copies = [
        pltpu.make_async_copy(source, target, w_sem.at[at])
        for at, (source, target) in enumerate(((wg_hbm, wg), (wu_hbm, wu), (wd_hbm, wd)))
    ]
    for copy in weight_copies:
        copy.start()

    barrier = pltpu.get_barrier_semaphore()
    for d in range(1, groups):
        pl.semaphore_signal(barrier, inc=1, device_id=at_g(low(my_g + d, groups)), device_id_type=MESH)
    for d in range(1, depth):
        pl.semaphore_signal(barrier, inc=1, device_id=at_z(low(my_z + d, depth)), device_id_type=MESH)
    for d in range(1, ring):
        pl.semaphore_signal(barrier, inc=1, device_id=at_x(low(my_x + d, ring)), device_id_type=MESH)
    pl.semaphore_wait(barrier, groups + depth + ring - 3)

    def spread(a):
        for d in range(1, groups):
            go(remote(tok_ref.at[a], got_a.at[a, my_g], a_send.at[a, d], a_recv.at[a, d], at_g(low(my_g + d, groups))))
        got_a[a, my_g] = tok_ref[a]

    spread(0)
    slot_rows = ring * ranks * slots
    token_rows = groups * pieces

    def slot_of(index):
        s = low(index, slots)
        token = jnp.full(index.shape, slot_ref[0], jnp.int32)
        for at in range(1, slots):
            token = jnp.where(s == at, slot_ref[at], token)
        rest = high(index, slots)
        piece = low(rest, ranks) * ring + high(rest, ranks)
        return token * pieces + piece

    shape = (slot_rows, token_rows)
    pick = onehot(
        slot_of(lax.broadcasted_iota(jnp.int32, shape, 0)) == lax.broadcasted_iota(jnp.int32, shape, 1)
    )
    shape = (token_rows, slot_rows)
    unpick = onehot(
        slot_of(lax.broadcasted_iota(jnp.int32, shape, 1)) == lax.broadcasted_iota(jnp.int32, shape, 0)
    )
    shape = (slot_rows, slot_rows)
    row = lax.broadcasted_iota(jnp.int32, shape, 0)
    rest = high(row, slots)
    turned = (low(rest, ring) * ranks + high(rest, ring)) * slots + low(row, slots)
    turn = onehot(lax.broadcasted_iota(jnp.int32, shape, 1) == turned)
    shape = (slot_rows, blocks * slot_rows)
    row = lax.broadcasted_iota(jnp.int32, shape, 0)
    rest = high(row, slots)
    turned = (low(rest, ranks) * ring + high(rest, ranks)) * slots + low(row, slots)
    fold = onehot(low(lax.broadcasted_iota(jnp.int32, shape, 1), slot_rows) == turned)

    def gather_tokens(a):
        for d in range(1, groups):
            slot = got_a.at[a, low(my_g - d, groups)]
            remote(slot, slot, a_send.at[a, d], a_recv.at[a, d], at_g(my_g)).wait_recv()

    def cross(a):
        chosen = exact_dot(pick, got_a[a].reshape(token_rows, width)).astype(jnp.bfloat16)
        sel[a] = chosen.reshape(ring, ranks * slots, width)
        for d in range(1, ring):
            to = low(my_x + d, ring)
            go(remote(sel.at[a, to], got_x.at[a, my_x], x_send.at[a, d], x_recv.at[a, d], at_x(to)))
        got_x[a, my_x] = sel[a, my_x]
        for d in range(1, ring):
            slot = got_x.at[a, low(my_x - d, ring)]
            remote(slot, slot, x_send.at[a, d], x_recv.at[a, d], at_x(my_x)).wait_recv()
        mixed = exact_dot(turn, got_x[a].reshape(slot_rows, width)).astype(jnp.bfloat16)
        blk[a] = mixed.reshape(ranks, chunk, width)

    def send_deep(a):
        for d in range(1, depth):
            to = low(my_z + d, depth)
            go(remote(blk.at[a, low(to, ranks)], rows.at[a, my_z], z_send.at[a, d], z_recv.at[a, d], at_z(to)))
        rows[a, my_z] = blk[a, my_r]

    def wait_deep(a):
        for d in range(1, depth):
            slot = rows.at[a, low(my_z - d, depth)]
            remote(slot, slot, z_send.at[a, d], z_recv.at[a, d], at_z(my_z)).wait_recv()

    def ring_send(q, value):
        part[q] = value.astype(jnp.bfloat16).reshape(ring, ranks * chunk, hidden)
        for d in range(1, ring):
            to = low(my_x + d, ring)
            go(remote(part.at[q, to], got_rx.at[q, d], rx_send.at[q, d], rx_recv.at[q, d], at_x(to)))

    def line_send(q):
        total = part[q, my_x].astype(jnp.float32)
        for d in range(1, ring):
            slot = got_rx.at[q, d]
            remote(slot, slot, rx_send.at[q, d], rx_recv.at[q, d], at_x(my_x)).wait_recv()
            total += got_rx[q, d].astype(jnp.float32)
        part_z[q] = total.astype(jnp.bfloat16).reshape(ranks, chunk, hidden)
        for d in range(1, ranks):
            to = low(my_r + d, ranks)
            go(remote(part_z.at[q, to], got_rz.at[q, d], rz_send.at[q, d], rz_recv.at[q, d], at_z(z_base + to)))

    def line_sum(q):
        total = part_z[q, my_r].astype(jnp.float32)
        for d in range(1, ranks):
            slot = got_rz.at[q, d]
            remote(slot, slot, rz_send.at[q, d], rz_recv.at[q, d], at_z(my_z)).wait_recv()
            total += got_rz[q, d].astype(jnp.float32)
        return total

    gather_tokens(0)
    spread(1)
    cross(0)
    send_deep(0)
    gather_tokens(1)
    cross(1)
    wait_deep(0)
    send_deep(1)
    rows_x = rows[0].reshape(depth * chunk, width)
    weight_copies[0].wait()
    ring_send(0, exact_dot(rows_x, wg[...]))
    weight_copies[1].wait()
    ring_send(1, exact_dot(rows_x, wu[...]))
    wait_deep(1)
    weight_copies[2].wait()
    ring_send(2, dot_nt(rows[1].reshape(depth * chunk, width), wd[...]))
    line_send(0)
    line_send(1)
    line_send(2)
    gate = line_sum(0)
    up = line_sum(1)
    back = line_sum(2) * rowp_ref[...]
    sig = 1.0 / (1.0 + jnp.exp(-gate))
    mine = my_x * ranks + my_r
    grads[mine, 0] = (back * up * sig * (1.0 + gate * (1.0 - sig))).astype(jnp.bfloat16)
    grads[mine, 1] = (back * gate * sig).astype(jnp.bfloat16)

    for d in range(1, ranks):
        to = z_base + low(my_r + d, ranks)
        go(remote(grads.at[mine], grads.at[mine], gz_send.at[d], gz_recv.at[d], at_z(to)))
    for d in range(1, ranks):
        slot = grads.at[my_x * ranks + low(my_r - d, ranks)]
        remote(slot, slot, gz_send.at[d], gz_recv.at[d], at_z(my_z)).wait_recv()
    held = grads.at[pl.ds(my_x * ranks, ranks)]
    for d in range(1, ring):
        go(remote(held, held, gx_send.at[d], gx_recv.at[d], at_x(low(my_x + d, ring))))

    for d in (0, 1, 3, 2) if ring == 4 else range(ring):
        owner = low(my_x - d, ring)
        first = owner * ranks
        if d:
            slot = grads.at[pl.ds(first, ranks)]
            remote(slot, slot, gx_send.at[d], gx_recv.at[d], at_x(my_x)).wait_recv()
        both = grads[pl.ds(first, ranks)]
        result = dot_nt(both[:, 0].reshape(ranks * chunk, hidden), wg[...])
        result += dot_nt(both[:, 1].reshape(ranks * chunk, hidden), wu[...])
        ret[pl.ds(first, ranks)] = result.astype(jnp.bfloat16).reshape(ranks, chunk, width)
        for j in range(ranks):
            to = first + j

            @pl.when(to != my_z)
            def _():
                remote(ret.at[to], got_ret.at[my_z], tz_send.at[to], tz_recv.at[my_z], at_z(to)).start()

    got_ret[my_z] = ret[my_z]
    for d in range(1, depth):
        source = low(my_z - d, depth)
        slot = got_ret.at[source]
        remote(slot, slot, tz_send.at[source], tz_recv.at[source], at_z(my_z)).wait_recv()
    folded = exact_dot(fold, got_ret[...].reshape(blocks * slot_rows, width)).astype(jnp.bfloat16)
    ret_x[...] = folded.reshape(ring, ranks * slots, width)
    for d in range(1, ring):
        to = low(my_x + d, ring)
        go(remote(ret_x.at[to], got_retx.at[my_x], tx_send.at[d], tx_recv.at[d], at_x(to)))
    got_retx[my_x] = ret_x[my_x]
    for d in range(1, ring):
        slot = got_retx.at[low(my_x - d, ring)]
        remote(slot, slot, tx_send.at[d], tx_recv.at[d], at_x(my_x)).wait_recv()
    spread_rows = exact_dot(unpick, got_retx[...].reshape(slot_rows, width)).astype(jnp.bfloat16)
    scat[...] = spread_rows.reshape(groups, pieces, width)
    for d in range(1, groups):
        to = low(my_g + d, groups)
        go(remote(scat.at[to], fin.at[d], tg_send.at[d], tg_recv.at[d], at_g(to)))
    total = scat[my_g].astype(jnp.float32)
    for d in range(1, groups):
        slot = fin.at[d]
        remote(slot, slot, tg_send.at[d], tg_recv.at[d], at_g(my_g)).wait_recv()
        total += fin[d].astype(jnp.float32)
    out_ref[...] = total.astype(jnp.bfloat16)

    for copy in sent:
        copy.wait_send()
    for d in range(1, depth):
        to = low(my_z + d, depth)
        remote(ret.at[to], got_ret.at[my_z], tz_send.at[to], tz_recv.at[my_z], at_z(to)).wait_send()


def run(sizes, slot_tokens, tokens, row_p, w_gate, w_up, w_down):
    groups, blocks, ranks, ring, slots = sizes
    depth, pieces, chunk = blocks * ranks, ranks * ring, ring * slots
    width, hidden = w_gate.shape
    bf = jnp.bfloat16
    vmem = functools.partial(pltpu.VMEM, dtype=bf)
    dma = pltpu.SemaphoreType.DMA
    any_spec = pl.BlockSpec(memory_space=pl.ANY)
    vmem_spec = pl.BlockSpec(memory_space=pltpu.VMEM)
    return pl.pallas_call(
        functools.partial(kernel, sizes),
        out_shape=jax.ShapeDtypeStruct((pieces, width), bf),
        in_specs=[pl.BlockSpec(memory_space=pltpu.SMEM), vmem_spec, vmem_spec, any_spec, any_spec, any_spec],
        out_specs=vmem_spec,
        scratch_shapes=[
            vmem((width, hidden)),
            vmem((width, hidden)),
            vmem((hidden, width)),
            vmem((2, groups, pieces, width)),
            vmem((2, ring, ranks * slots, width)),
            vmem((2, ring, ranks * slots, width)),
            vmem((2, ranks, chunk, width)),
            vmem((2, depth, chunk, width)),
            vmem((3, ring, ranks * chunk, hidden)),
            vmem((3, ring, ranks * chunk, hidden)),
            vmem((3, ranks, chunk, hidden)),
            vmem((3, ranks, chunk, hidden)),
            vmem((depth, 2, chunk, hidden)),
            vmem((depth, chunk, width)),
            vmem((depth, chunk, width)),
            vmem((ring, ranks * slots, width)),
            vmem((ring, ranks * slots, width)),
            vmem((groups, pieces, width)),
            vmem((groups, pieces, width)),
            dma((3,)),
            dma((2, groups)),
            dma((2, groups)),
            dma((2, ring)),
            dma((2, ring)),
            dma((2, depth)),
            dma((2, depth)),
            dma((3, ring)),
            dma((3, ring)),
            dma((3, ranks)),
            dma((3, ranks)),
            dma((ranks,)),
            dma((ranks,)),
            dma((ring,)),
            dma((ring,)),
            dma((depth,)),
            dma((depth,)),
            dma((ring,)),
            dma((ring,)),
            dma((groups,)),
            dma((groups,)),
        ],
        compiler_params=pltpu.CompilerParams(
            collective_id=0, has_side_effects=True, vmem_limit_bytes=40 * 1024 * 1024
        ),
    )(slot_tokens, tokens, row_p, w_gate, w_up, w_down)


def slot_maps(named):
    tokens = named.shape[0]
    order = jnp.arange(tokens, dtype=jnp.int32)
    ahead = (order[:, None] > order[None, :]).astype(jnp.int32)
    before = jnp.sum(
        ahead.reshape((tokens, tokens) + (1,) * (named.ndim - 1)) * named[None].astype(jnp.int32), axis=1
    )
    return named[..., None] & (before[..., None] == jnp.arange(SLOTS, dtype=jnp.int32))


def on_device(x_rows, grad_rows, routes, probs, w_gate, w_up, w_down, sizes):
    groups, blocks, ranks, ring, slots = sizes
    my_g = lax.axis_index("group")
    my_e = lax.axis_index("expert")
    my_z, my_x = my_e // ring, my_e % ring
    width = w_gate.shape[1]
    pieces = ranks * ring
    tokens = jnp.stack([x_rows.reshape(pieces, width), grad_rows.reshape(pieces, width)])
    column = lax.dynamic_slice_in_dim(routes, my_e, 1, 1)[:, 0, 0]
    mask = slot_maps(jnp.any(column // blocks == my_g, axis=1))
    slot_tokens = jnp.sum(mask * jnp.arange(groups, dtype=jnp.int32)[:, None], axis=0)
    owned = (my_x * ranks + my_z % ranks) * ring
    near = lax.dynamic_slice_in_dim(routes, owned, ring, 1)[:, :, 0]
    near_p = lax.dynamic_slice_in_dim(probs, owned, ring, 1)[:, :, 0].astype(jnp.float32)
    expert = my_g * blocks + my_z // ranks
    mask = slot_maps(jnp.any(near // blocks == my_g, axis=2))
    weight = jnp.sum(jnp.where(near == expert, near_p, 0.0), axis=2)
    row_p = jnp.sum(jnp.where(mask, weight[:, :, None], 0.0), axis=0).reshape(ring * slots, 1)
    result = run(sizes, slot_tokens, tokens, row_p, w_gate[0], w_up[0], w_down[0])
    return result.reshape(x_rows.shape)


def solution(mesh):
    sizes = (mesh.shape["group"], BLOCKS, RANKS, RING, SLOTS)
    in_specs = (
        P("group", "expert", None, None),
        P("group", "expert", None, None),
        P(),
        P(),
        P(("group", "expert"), None, None),
        P(("group", "expert"), None, None),
        P(("group", "expert"), None, None),
    )
    return jax.shard_map(
        functools.partial(on_device, sizes=sizes),
        mesh=mesh,
        in_specs=in_specs,
        out_specs=P("group", "expert", None, None),
        check_vma=False,
    )
```

```python
import functools

import jax
import jax.numpy as jnp
from jax import lax
from jax.experimental import pallas as pl
from jax.experimental.pallas import tpu as pltpu
from jax.sharding import PartitionSpec as P

MESH = pl.DeviceIdType.MESH
BLOCKS = 4
RANKS = 4
RING = 4
SLOTS = 4


def low(value, size):
    return value & (size - 1)


def high(value, size):
    return value >> (size.bit_length() - 1)


def onehot(mask):
    return jnp.where(mask, 1.0, 0.0).astype(jnp.bfloat16)


def exact_dot(left, right):
    return jnp.dot(left, right, preferred_element_type=jnp.float32)


def dot_nt(left, right):
    return lax.dot_general(left, right, (((1,), (1,)), ((), ())), preferred_element_type=jnp.float32)


def kernel(
    sizes,
    tok_ref,
    route_ref,
    prob_ref,
    wg_hbm,
    wu_hbm,
    wd_hbm,
    out_ref,
    wg,
    wu,
    wd,
    pair,
    got_a,
    got_b,
    sel,
    sel_b,
    got_x,
    got_xb,
    blk,
    blk_b,
    rows,
    rows_b,
    part,
    got_rx,
    part_z,
    got_rz,
    grads,
    ret,
    got_ret,
    ret_x,
    got_retx,
    scat,
    fin,
    w_sem,
    p_send,
    p_recv,
    a_send,
    a_recv,
    c_send,
    c_recv,
    x_send,
    x_recv,
    z_send,
    z_recv,
    rx_send,
    rx_recv,
    rz_send,
    rz_recv,
    gz_send,
    gz_recv,
    gx_send,
    gx_recv,
    tz_send,
    tz_recv,
    tx_send,
    tx_recv,
    tg_send,
    tg_recv,
):
    groups, blocks, ranks, ring, slots = sizes
    depth = blocks * ranks
    pieces = ranks * ring
    chunk = ring * slots
    lines = groups // 2
    half = depth // 2
    width = tok_ref.shape[2]
    hidden = wg.shape[1]
    my_g = lax.axis_index("group")
    my_e = lax.axis_index("expert")
    my_x = low(my_e, ring)
    my_z = high(my_e, ring)
    my_r = low(my_z, ranks)
    z_base = my_z - my_r
    my_core = low(my_g, 2)
    my_y = high(my_g, 2)
    my_half = high(my_z, half)

    def chunk_of(z):
        return low(z, half) * 2 + high(z, half)

    def z_of(at):
        return low(at, 2) * half + high(at, 2)

    def at_x(x):
        return (my_g, my_z * ring + x)

    def at_z(z):
        return (my_g, z * ring + my_x)

    def at_g(g):
        return (g, my_e)

    def remote(src, dst, send, recv, device):
        return pltpu.make_async_remote_copy(
            src_ref=src, dst_ref=dst, send_sem=send, recv_sem=recv, device_id=device, device_id_type=MESH
        )

    around = sorted(range(1, ring), key=lambda d: min(d, ring - d))
    sent = []

    def go(copy):
        copy.start()
        sent.append(copy)

    weight_copies = [
        pltpu.make_async_copy(source, target, w_sem.at[at])
        for at, (source, target) in enumerate(((wg_hbm, wg), (wu_hbm, wu), (wd_hbm, wd)))
    ]
    for copy in weight_copies:
        copy.start()

    barrier = pltpu.get_barrier_semaphore()
    for d in range(1, groups):
        pl.semaphore_signal(barrier, inc=1, device_id=at_g(low(my_g + d, groups)), device_id_type=MESH)
    for d in range(1, depth):
        pl.semaphore_signal(barrier, inc=1, device_id=at_z(low(my_z + d, depth)), device_id_type=MESH)
    for d in range(1, ring):
        pl.semaphore_signal(barrier, inc=1, device_id=at_x(low(my_x + d, ring)), device_id_type=MESH)

    slot_rows = ring * ranks * slots
    token_rows = groups * pieces

    route = route_ref[...]
    columns = route.shape[2]
    in_group = jnp.max(jnp.where(high(route, blocks) == my_g, 1.0, 0.0), axis=1)
    expert = my_g * blocks + high(my_z, ranks)
    weight = jnp.sum(jnp.where(route == expert, prob_ref[...].astype(jnp.float32), 0.0), axis=1)
    lane = lax.broadcasted_iota(jnp.int32, (1, columns), 1)
    count = jnp.zeros((1, columns), jnp.float32)
    slot_token = [count] * slots
    slot_weight = [count] * slots
    for m in range(groups):
        named = in_group[m : m + 1]
        for s in range(slots):
            here = jnp.where(count == s, named, 0.0)
            slot_token[s] += here * (m % 2 * lines + m // 2)
            slot_weight[s] += here * weight[m : m + 1]
        count += named

    def tokens_of(column):
        return [
            jnp.sum(jnp.where(lane == column, token, 0.0), axis=1, keepdims=True).astype(jnp.int32)
            for token in slot_token
        ]

    my_tokens = tokens_of(my_e)
    pair_tokens = [tokens_of((h * half + low(my_z, half)) * ring + my_x) for h in range(2)]
    row = lax.broadcasted_iota(jnp.int32, (chunk, columns), 0)
    owned = z_of(my_x * ranks + my_r) * ring
    row_p = jnp.zeros((chunk, columns), jnp.float32)
    for s in range(slots):
        row_p = jnp.where(low(row, slots) == s, slot_weight[s], row_p)
    owner = owned + high(row, slots) == lax.broadcasted_iota(jnp.int32, (chunk, columns), 1)
    row_p = jnp.sum(jnp.where(owner, row_p, 0.0), axis=1, keepdims=True)

    def slot_of(index, tokens):
        s = low(index, slots)
        token = jnp.broadcast_to(tokens[0], index.shape)
        for at in range(1, slots):
            token = jnp.where(s == at, tokens[at], token)
        rest = high(index, slots)
        piece = low(rest, ranks) * ring + high(rest, ranks)
        return token * pieces + piece

    def picking(tokens):
        shape = (slot_rows, token_rows)
        return onehot(
            slot_of(lax.broadcasted_iota(jnp.int32, shape, 0), tokens)
            == lax.broadcasted_iota(jnp.int32, shape, 1)
        )

    shape = (token_rows, slot_rows)
    unpick = onehot(
        slot_of(lax.broadcasted_iota(jnp.int32, shape, 1), my_tokens)
        == lax.broadcasted_iota(jnp.int32, shape, 0)
    )
    picks = [picking(my_tokens)] + [picking(tokens) for tokens in pair_tokens]
    shape = (slot_rows, slot_rows)
    row = lax.broadcasted_iota(jnp.int32, shape, 0)
    rest = high(row, slots)
    turned = (low(rest, ring) * ranks + high(rest, ring)) * slots + low(row, slots)
    turn = onehot(lax.broadcasted_iota(jnp.int32, shape, 1) == turned)
    shape = (slot_rows, blocks * slot_rows)
    row = lax.broadcasted_iota(jnp.int32, shape, 0)
    rest = high(row, slots)
    turned = (low(rest, ranks) * ring + high(rest, ranks)) * slots + low(row, slots)
    fold = onehot(low(lax.broadcasted_iota(jnp.int32, shape, 1), slot_rows) == turned)

    pl.semaphore_wait(barrier, groups + depth + ring - 3)

    far_first = sorted(range(1, lines), key=lambda d: -min(d, lines - d))

    def spread(a, source, target):
        for d in far_first:
            to = low(my_y + d, lines) * 2 + my_core
            go(remote(source, target.at[my_core, my_y], a_send.at[a, d], a_recv.at[a, d], at_g(to)))
        target[my_core, my_y] = source[...]

    def share(a, target):
        for d in range(1, lines):
            slot = target.at[my_core, low(my_y - d, lines)]
            remote(slot, slot, a_send.at[a, d], a_recv.at[a, d], at_g(my_g)).wait_recv()
        mine = target.at[my_core]
        go(remote(mine, mine, c_send.at[a], c_recv.at[a], at_g(my_y * 2 + 1 - my_core)))

    def wait_share(a, target):
        slot = target.at[1 - my_core]
        remote(slot, slot, c_send.at[a], c_recv.at[a], at_g(my_g)).wait_recv()

    def ring_swap(a, source, target):
        for d in range(1, ring):
            to = low(my_x + d, ring)
            go(remote(source.at[to], target.at[my_x], x_send.at[a, d], x_recv.at[a, d], at_x(to)))
        target[my_x] = source[my_x]

    def wait_swap(a, target):
        for d in range(1, ring):
            slot = target.at[low(my_x - d, ring)]
            remote(slot, slot, x_send.at[a, d], x_recv.at[a, d], at_x(my_x)).wait_recv()

    near = list(range(1, depth // 4 + 1)) + list(range(depth - depth // 4 + 1, depth))
    near.sort(key=lambda d: min(d, depth - d))
    all_z = sorted(range(1, depth), key=lambda d: min(d, depth - d))

    way = 1 - 2 * my_core

    def send_deep(a, steps, source, slot):
        for d in steps:
            to = low(my_z + way * d, depth)
            go(remote(source.at[low(to, ranks)], slot, z_send.at[a, d], z_recv.at[a, d], at_z(to)))
        slot[...] = source[my_r]

    def wait_deep(a, steps, slot_from):
        for d in steps:
            slot = slot_from(low(my_z - way * d, depth))
            remote(slot, slot, z_send.at[a, d], z_recv.at[a, d], at_z(my_z)).wait_recv()

    def ring_send(q, value):
        part[q] = value.astype(jnp.bfloat16).reshape(ring, ranks * chunk, hidden)
        for d in around:
            to = low(my_x + d, ring)
            go(remote(part.at[q, to], got_rx.at[q, d], rx_send.at[q, d], rx_recv.at[q, d], at_x(to)))

    def line_send(q):
        total = part[q, my_x].astype(jnp.float32)
        for d in range(1, ring):
            slot = got_rx.at[q, d]
            remote(slot, slot, rx_send.at[q, d], rx_recv.at[q, d], at_x(my_x)).wait_recv()
            total += got_rx[q, d].astype(jnp.float32)
        part_z[q] = total.astype(jnp.bfloat16).reshape(ranks, chunk, hidden)
        for d in range(1, ranks):
            to = low(my_r + d, ranks)
            go(remote(part_z.at[q, to], got_rz.at[q, d], rz_send.at[q, d], rz_recv.at[q, d], at_z(z_base + to)))

    def line_sum(q):
        total = part_z[q, my_r].astype(jnp.float32)
        for d in range(1, ranks):
            slot = got_rz.at[q, d]
            remote(slot, slot, rz_send.at[q, d], rz_recv.at[q, d], at_z(my_z)).wait_recv()
            total += got_rz[q, d].astype(jnp.float32)
        return total

    spread(0, tok_ref.at[0], got_a)
    go(remote(tok_ref.at[1], pair.at[my_half], p_send, p_recv, at_z(low(my_z + half, depth))))
    pair[my_half] = tok_ref[1]
    share(0, got_a)
    slot = pair.at[1 - my_half]
    remote(slot, slot, p_send, p_recv, at_z(my_z)).wait_recv()
    spread(1, pair, got_b)
    wait_share(0, got_a)
    chosen = exact_dot(picks[0], got_a[...].reshape(token_rows, width)).astype(jnp.bfloat16)
    sel[...] = chosen.reshape(ring, ranks * slots, width)
    ring_swap(0, sel, got_x)
    wait_swap(0, got_x)
    mixed = exact_dot(turn, got_x[...].reshape(slot_rows, width)).astype(jnp.bfloat16)
    blk[...] = mixed.reshape(ranks, chunk, width)
    send_deep(0, all_z, blk, rows.at[chunk_of(my_z)])
    share(1, got_b)
    wait_share(1, got_b)
    for h in range(2):
        chosen = exact_dot(picks[1 + h], got_b[:, :, h].reshape(token_rows, width)).astype(jnp.bfloat16)
        sel_b[:, h] = chosen.reshape(ring, ranks * slots, width)
    ring_swap(1, sel_b, got_xb)
    wait_swap(1, got_xb)
    for h in range(2):
        mixed = exact_dot(turn, got_xb[:, h].reshape(slot_rows, width)).astype(jnp.bfloat16)
        blk_b[:, h] = mixed.reshape(ranks, chunk, width)
    send_deep(1, near, blk_b, rows_b.at[low(my_z, half)])
    wait_deep(0, all_z, lambda z: rows.at[chunk_of(z)])
    rows_x = rows[...].reshape(depth * chunk, width)
    weight_copies[0].wait()
    ring_send(0, exact_dot(rows_x, wg[...]))
    weight_copies[1].wait()
    ring_send(1, exact_dot(rows_x, wu[...]))
    wait_deep(1, near, lambda z: rows_b.at[low(z, half)])
    weight_copies[2].wait()
    ring_send(2, exact_dot(rows_b[...].reshape(depth * chunk, width), wd[...]))
    line_send(0)
    line_send(1)
    line_send(2)
    gate = line_sum(0)
    up = line_sum(1)
    back = line_sum(2) * row_p
    sig = 1.0 / (1.0 + jnp.exp(-gate))
    mine = my_x * ranks + my_r
    grads[mine, 0] = (back * up * sig * (1.0 + gate * (1.0 - sig))).astype(jnp.bfloat16)
    grads[mine, 1] = (back * gate * sig).astype(jnp.bfloat16)

    for d in range(1, ranks):
        to = z_base + low(my_r + d, ranks)
        go(remote(grads.at[mine], grads.at[mine], gz_send.at[d], gz_recv.at[d], at_z(to)))
    for d in range(1, ranks):
        slot = grads.at[my_x * ranks + low(my_r - d, ranks)]
        remote(slot, slot, gz_send.at[d], gz_recv.at[d], at_z(my_z)).wait_recv()
    held = grads.at[pl.ds(my_x * ranks, ranks)]
    for d in around:
        go(remote(held, held, gx_send.at[d], gx_recv.at[d], at_x(low(my_x + d, ring))))

    for d in [0] + around:
        owner = low(my_x - d, ring)
        first = owner * ranks
        if d:
            slot = grads.at[pl.ds(first, ranks)]
            remote(slot, slot, gx_send.at[d], gx_recv.at[d], at_x(my_x)).wait_recv()
        both = grads[pl.ds(first, ranks)]
        result = dot_nt(both[:, 0].reshape(ranks * chunk, hidden), wg[...])
        result += dot_nt(both[:, 1].reshape(ranks * chunk, hidden), wu[...])
        ret[pl.ds(first, ranks)] = result.astype(jnp.bfloat16).reshape(ranks, chunk, width)
        for j in range(ranks):
            at = first + j
            to = z_of(at)

            @pl.when(to != my_z)
            def _(at=at, to=to):
                remote(ret.at[at], got_ret.at[my_z], tz_send.at[to], tz_recv.at[my_z], at_z(to)).start()

    got_ret[my_z] = ret[chunk_of(my_z)]
    for d in range(1, depth):
        source = low(my_z - d, depth)
        slot = got_ret.at[source]
        remote(slot, slot, tz_send.at[source], tz_recv.at[source], at_z(my_z)).wait_recv()
    folded = exact_dot(fold, got_ret[...].reshape(blocks * slot_rows, width)).astype(jnp.bfloat16)
    ret_x[...] = folded.reshape(ring, ranks * slots, width)
    for d in range(1, ring):
        to = low(my_x + d, ring)
        go(remote(ret_x.at[to], got_retx.at[my_x], tx_send.at[d], tx_recv.at[d], at_x(to)))
    got_retx[my_x] = ret_x[my_x]
    for d in range(1, ring):
        slot = got_retx.at[low(my_x - d, ring)]
        remote(slot, slot, tx_send.at[d], tx_recv.at[d], at_x(my_x)).wait_recv()
    spread_rows = exact_dot(unpick, got_retx[...].reshape(slot_rows, width)).astype(jnp.bfloat16)
    scat[...] = spread_rows.reshape(groups, pieces, width)
    for d in range(1, groups):
        to = low(my_g + d, groups)
        go(remote(scat.at[low(to, 2) * lines + high(to, 2)], fin.at[d], tg_send.at[d], tg_recv.at[d], at_g(to)))
    total = scat[low(my_g, 2) * lines + high(my_g, 2)].astype(jnp.float32)
    for d in range(1, groups):
        slot = fin.at[d]
        remote(slot, slot, tg_send.at[d], tg_recv.at[d], at_g(my_g)).wait_recv()
        total += fin[d].astype(jnp.float32)
    out_ref[...] = total.astype(jnp.bfloat16)

    for copy in sent:
        copy.wait_send()
    for d in range(1, depth):
        to = low(my_z + d, depth)
        remote(ret.at[chunk_of(to)], got_ret.at[my_z], tz_send.at[to], tz_recv.at[my_z], at_z(to)).wait_send()


def run(sizes, tokens, routes, probs, w_gate, w_up, w_down):
    groups, blocks, ranks, ring, slots = sizes
    depth, pieces, chunk = blocks * ranks, ranks * ring, ring * slots
    width, hidden = w_gate.shape
    bf = jnp.bfloat16
    vmem = functools.partial(pltpu.VMEM, dtype=bf)
    dma = pltpu.SemaphoreType.DMA
    any_spec = pl.BlockSpec(memory_space=pl.ANY)
    vmem_spec = pl.BlockSpec(memory_space=pltpu.VMEM)
    return pl.pallas_call(
        functools.partial(kernel, sizes),
        out_shape=jax.ShapeDtypeStruct((pieces, width), bf),
        in_specs=[vmem_spec, vmem_spec, vmem_spec, any_spec, any_spec, any_spec],
        out_specs=vmem_spec,
        scratch_shapes=[
            vmem((width, hidden)),
            vmem((width, hidden)),
            vmem((width, hidden)),
            vmem((2, pieces, width)),
            vmem((2, groups // 2, pieces, width)),
            vmem((2, groups // 2, 2, pieces, width)),
            vmem((ring, ranks * slots, width)),
            vmem((ring, 2, ranks * slots, width)),
            vmem((ring, ranks * slots, width)),
            vmem((ring, 2, ranks * slots, width)),
            vmem((ranks, chunk, width)),
            vmem((ranks, 2, chunk, width)),
            vmem((depth, chunk, width)),
            vmem((depth // 2, 2, chunk, width)),
            vmem((3, ring, ranks * chunk, hidden)),
            vmem((3, ring, ranks * chunk, hidden)),
            vmem((3, ranks, chunk, hidden)),
            vmem((3, ranks, chunk, hidden)),
            vmem((depth, 2, chunk, hidden)),
            vmem((depth, chunk, width)),
            vmem((depth, chunk, width)),
            vmem((ring, ranks * slots, width)),
            vmem((ring, ranks * slots, width)),
            vmem((groups, pieces, width)),
            vmem((groups, pieces, width)),
            dma((3,)),
            dma(()),
            dma(()),
            dma((2, groups // 2)),
            dma((2, groups // 2)),
            dma((2,)),
            dma((2,)),
            dma((2, ring)),
            dma((2, ring)),
            dma((2, depth)),
            dma((2, depth)),
            dma((3, ring)),
            dma((3, ring)),
            dma((3, ranks)),
            dma((3, ranks)),
            dma((ranks,)),
            dma((ranks,)),
            dma((ring,)),
            dma((ring,)),
            dma((depth,)),
            dma((depth,)),
            dma((ring,)),
            dma((ring,)),
            dma((groups,)),
            dma((groups,)),
        ],
        compiler_params=pltpu.CompilerParams(
            collective_id=0, has_side_effects=True, vmem_limit_bytes=40 * 1024 * 1024
        ),
    )(tokens, routes, probs, w_gate, w_up, w_down)


def on_device(x_rows, grad_rows, routes, probs, w_gate, w_up, w_down, sizes):
    groups, blocks, ranks, ring, slots = sizes
    pieces, width = ranks * ring, w_gate.shape[1]
    tokens = jnp.stack([x_rows.reshape(pieces, width), grad_rows.reshape(pieces, width)])
    by_column = [jnp.swapaxes(array[:, :, 0], 1, 2) for array in (routes, probs)]
    result = run(sizes, tokens, *by_column, w_gate[0], w_up[0], jnp.swapaxes(w_down[0], 0, 1))
    return result.reshape(x_rows.shape)


def solution(mesh):
    sizes = (mesh.shape["group"], BLOCKS, RANKS, RING, SLOTS)
    in_specs = (
        P("group", "expert", None, None),
        P("group", "expert", None, None),
        P(),
        P(),
        P(("group", "expert"), None, None),
        P(("group", "expert"), None, None),
        P(("group", "expert"), None, None),
    )
    return jax.shard_map(
        functools.partial(on_device, sizes=sizes),
        mesh=mesh,
        in_specs=in_specs,
        out_specs=P("group", "expert", None, None),
        check_vma=False,
    )
```

```python
import functools

import jax
import jax.numpy as jnp
from jax import lax
from jax.experimental import pallas as pl
from jax.experimental.pallas import tpu as pltpu
from jax.sharding import PartitionSpec as P

MESH = pl.DeviceIdType.MESH
BLOCKS = 4
RANKS = 4
RING = 4
SLOTS = 4


def low(value, size):
    return value & (size - 1)


def high(value, size):
    return value >> (size.bit_length() - 1)


def onehot(mask):
    return jnp.where(mask, 1.0, 0.0).astype(jnp.bfloat16)


def exact_dot(left, right):
    return jnp.dot(left, right, preferred_element_type=jnp.float32)


def dot_nt(left, right):
    return lax.dot_general(left, right, (((1,), (1,)), ((), ())), preferred_element_type=jnp.float32)


def kernel(
    sizes,
    tok_ref,
    route_hbm,
    prob_hbm,
    wg_hbm,
    wu_hbm,
    wd_hbm,
    out_ref,
    route_ref,
    prob_ref,
    wg,
    wu,
    wd,
    pair,
    got_a,
    got_b,
    sel,
    sel_b,
    got_x,
    got_xb,
    blk,
    blk_b,
    rows,
    rows_b,
    part,
    got_rx,
    part_z,
    got_rz,
    part_zb,
    got_zb,
    part_xb,
    got_rxb,
    grads,
    ret,
    got_ret,
    ret_x,
    got_retx,
    scat,
    fin,
    w_sem,
    m_sem,
    p_send,
    p_recv,
    a_send,
    a_recv,
    c_send,
    c_recv,
    x_send,
    x_recv,
    z_send,
    z_recv,
    rx_send,
    rx_recv,
    rz_send,
    rz_recv,
    bz_send,
    bz_recv,
    bx_send,
    bx_recv,
    gz_send,
    gz_recv,
    gx_send,
    gx_recv,
    tz_send,
    tz_recv,
    tx_send,
    tx_recv,
    tg_send,
    tg_recv,
):
    groups, blocks, ranks, ring, slots = sizes
    depth = blocks * ranks
    pieces = ranks * ring
    chunk = ring * slots
    lines = groups // 2
    half = depth // 2
    width = tok_ref.shape[2]
    hidden = wg.shape[1]
    my_g = lax.axis_index("group")
    my_e = lax.axis_index("expert")
    my_x = low(my_e, ring)
    my_z = high(my_e, ring)
    my_r = low(my_z, ranks)
    z_base = my_z - my_r
    my_core = low(my_g, 2)
    my_y = high(my_g, 2)
    my_half = high(my_z, half)

    def chunk_of(z):
        return low(z, half) * 2 + high(z, half)

    def z_of(at):
        return low(at, 2) * half + high(at, 2)

    def at_x(x):
        return (my_g, my_z * ring + x)

    def at_z(z):
        return (my_g, z * ring + my_x)

    def at_g(g):
        return (g, my_e)

    def remote(src, dst, send, recv, device):
        return pltpu.make_async_remote_copy(
            src_ref=src, dst_ref=dst, send_sem=send, recv_sem=recv, device_id=device, device_id_type=MESH
        )

    around = sorted(range(1, ring), key=lambda d: min(d, ring - d))
    sent = []

    def go(copy):
        copy.start()
        sent.append(copy)

    map_copies = [
        pltpu.make_async_copy(source, target, m_sem.at[at])
        for at, (source, target) in enumerate(((route_hbm, route_ref), (prob_hbm, prob_ref)))
    ]
    for copy in map_copies:
        copy.start()
    weight_copies = [
        pltpu.make_async_copy(source, target, w_sem.at[at])
        for at, (source, target) in enumerate(((wg_hbm, wg), (wu_hbm, wu), (wd_hbm, wd)))
    ]
    for copy in weight_copies:
        copy.start()

    barrier = pltpu.get_barrier_semaphore()
    for d in range(1, groups):
        pl.semaphore_signal(barrier, inc=1, device_id=at_g(low(my_g + d, groups)), device_id_type=MESH)
    for d in range(1, depth):
        pl.semaphore_signal(barrier, inc=1, device_id=at_z(low(my_z + d, depth)), device_id_type=MESH)
    for d in range(1, ring):
        pl.semaphore_signal(barrier, inc=1, device_id=at_x(low(my_x + d, ring)), device_id_type=MESH)

    slot_rows = ring * ranks * slots
    token_rows = groups * pieces

    for copy in map_copies:
        copy.wait()
    route = route_ref[...]
    columns = route.shape[2]
    in_group = jnp.max(jnp.where(high(route, blocks) == my_g, 1.0, 0.0), axis=1)
    expert = my_g * blocks + high(my_z, ranks)
    weight = jnp.sum(jnp.where(route == expert, prob_ref[...].astype(jnp.float32), 0.0), axis=1)
    lane = lax.broadcasted_iota(jnp.int32, (1, columns), 1)
    count = jnp.zeros((1, columns), jnp.float32)
    slot_token = [count] * slots
    slot_weight = [count] * slots
    for m in range(groups):
        named = in_group[m : m + 1]
        for s in range(slots):
            here = jnp.where(count == s, named, 0.0)
            slot_token[s] += here * (m % 2 * lines + m // 2)
            slot_weight[s] += here * weight[m : m + 1]
        count += named

    def tokens_of(column):
        return [
            jnp.sum(jnp.where(lane == column, token, 0.0), axis=1, keepdims=True).astype(jnp.int32)
            for token in slot_token
        ]

    my_tokens = tokens_of(my_e)
    pair_tokens = [tokens_of((h * half + low(my_z, half)) * ring + my_x) for h in range(2)]
    row = lax.broadcasted_iota(jnp.int32, (chunk, columns), 0)
    owned = z_of(my_x * ranks + my_r) * ring
    row_p = jnp.zeros((chunk, columns), jnp.float32)
    for s in range(slots):
        row_p = jnp.where(low(row, slots) == s, slot_weight[s], row_p)
    owner = owned + high(row, slots) == lax.broadcasted_iota(jnp.int32, (chunk, columns), 1)
    row_p = jnp.sum(jnp.where(owner, row_p, 0.0), axis=1, keepdims=True)

    def slot_of(index, tokens):
        s = low(index, slots)
        token = jnp.broadcast_to(tokens[0], index.shape)
        for at in range(1, slots):
            token = jnp.where(s == at, tokens[at], token)
        rest = high(index, slots)
        piece = low(rest, ranks) * ring + high(rest, ranks)
        return token * pieces + piece

    def picking(tokens):
        shape = (slot_rows, token_rows)
        return onehot(
            slot_of(lax.broadcasted_iota(jnp.int32, shape, 0), tokens)
            == lax.broadcasted_iota(jnp.int32, shape, 1)
        )

    shape = (token_rows, slot_rows)
    unpick = onehot(
        slot_of(lax.broadcasted_iota(jnp.int32, shape, 1), my_tokens)
        == lax.broadcasted_iota(jnp.int32, shape, 0)
    )
    picks = [picking(my_tokens)] + [picking(tokens) for tokens in pair_tokens]
    shape = (slot_rows, slot_rows)
    row = lax.broadcasted_iota(jnp.int32, shape, 0)
    rest = high(row, slots)
    turned = (low(rest, ring) * ranks + high(rest, ring)) * slots + low(row, slots)
    turn = onehot(lax.broadcasted_iota(jnp.int32, shape, 1) == turned)
    shape = (slot_rows, blocks * slot_rows)
    row = lax.broadcasted_iota(jnp.int32, shape, 0)
    rest = high(row, slots)
    turned = (low(rest, ranks) * ring + high(rest, ranks)) * slots + low(row, slots)
    fold = onehot(low(lax.broadcasted_iota(jnp.int32, shape, 1), slot_rows) == turned)

    pl.semaphore_wait(barrier, groups + depth + ring - 3)

    far_first = sorted(range(1, lines), key=lambda d: -min(d, lines - d))

    def spread(a, source, target):
        for d in far_first:
            to = low(my_y + d, lines) * 2 + my_core
            go(remote(source, target.at[my_core, my_y], a_send.at[a, d], a_recv.at[a, d], at_g(to)))
        target[my_core, my_y] = source[...]

    def share(a, target):
        for d in range(1, lines):
            slot = target.at[my_core, low(my_y - d, lines)]
            remote(slot, slot, a_send.at[a, d], a_recv.at[a, d], at_g(my_g)).wait_recv()
        mine = target.at[my_core]
        go(remote(mine, mine, c_send.at[a], c_recv.at[a], at_g(my_y * 2 + 1 - my_core)))

    def wait_share(a, target):
        slot = target.at[1 - my_core]
        remote(slot, slot, c_send.at[a], c_recv.at[a], at_g(my_g)).wait_recv()

    def ring_swap(a, source, target):
        for d in range(1, ring):
            to = low(my_x + d, ring)
            go(remote(source.at[to], target.at[my_x], x_send.at[a, d], x_recv.at[a, d], at_x(to)))
        target[my_x] = source[my_x]

    def wait_swap(a, target):
        for d in range(1, ring):
            slot = target.at[low(my_x - d, ring)]
            remote(slot, slot, x_send.at[a, d], x_recv.at[a, d], at_x(my_x)).wait_recv()

    near = list(range(1, depth // 4 + 1)) + list(range(depth - depth // 4 + 1, depth))
    near.sort(key=lambda d: min(d, depth - d))
    all_z = sorted(range(1, depth), key=lambda d: min(d, depth - d))

    way = 1 - 2 * my_core

    def send_deep(a, steps, source, slot):
        for d in steps:
            to = low(my_z + way * d, depth)
            go(remote(source.at[low(to, ranks)], slot, z_send.at[a, d], z_recv.at[a, d], at_z(to)))
        slot[...] = source[my_r]

    def wait_deep(a, steps, slot_from):
        for d in steps:
            slot = slot_from(low(my_z - way * d, depth))
            remote(slot, slot, z_send.at[a, d], z_recv.at[a, d], at_z(my_z)).wait_recv()

    def ring_send(q, value):
        part[q] = value.astype(jnp.bfloat16).reshape(ring, ranks * chunk, hidden)
        for d in around:
            to = low(my_x + d, ring)
            go(remote(part.at[q, to], got_rx.at[q, d], rx_send.at[q, d], rx_recv.at[q, d], at_x(to)))

    def line_send(q):
        total = part[q, my_x].astype(jnp.float32)
        for d in range(1, ring):
            slot = got_rx.at[q, d]
            remote(slot, slot, rx_send.at[q, d], rx_recv.at[q, d], at_x(my_x)).wait_recv()
            total += got_rx[q, d].astype(jnp.float32)
        part_z[q] = total.astype(jnp.bfloat16).reshape(ranks, chunk, hidden)
        for d in range(1, ranks):
            to = low(my_r + d, ranks)
            go(remote(part_z.at[q, to], got_rz.at[q, d], rz_send.at[q, d], rz_recv.at[q, d], at_z(z_base + to)))

    def line_sum(q):
        total = part_z[q, my_r].astype(jnp.float32)
        for d in range(1, ranks):
            slot = got_rz.at[q, d]
            remote(slot, slot, rz_send.at[q, d], rz_recv.at[q, d], at_z(my_z)).wait_recv()
            total += got_rz[q, d].astype(jnp.float32)
        return total

    spread(0, tok_ref.at[0], got_a)
    go(remote(tok_ref.at[1], pair.at[my_half], p_send, p_recv, at_z(low(my_z + half, depth))))
    pair[my_half] = tok_ref[1]
    share(0, got_a)
    slot = pair.at[1 - my_half]
    remote(slot, slot, p_send, p_recv, at_z(my_z)).wait_recv()
    spread(1, pair, got_b)
    wait_share(0, got_a)
    chosen = exact_dot(picks[0], got_a[...].reshape(token_rows, width)).astype(jnp.bfloat16)
    sel[...] = chosen.reshape(ring, ranks * slots, width)
    ring_swap(0, sel, got_x)
    wait_swap(0, got_x)
    mixed = exact_dot(turn, got_x[...].reshape(slot_rows, width)).astype(jnp.bfloat16)
    blk[...] = mixed.reshape(ranks, chunk, width)
    send_deep(0, all_z, blk, rows.at[chunk_of(my_z)])
    share(1, got_b)
    wait_share(1, got_b)
    for h in range(2):
        chosen = exact_dot(picks[1 + h], got_b[:, :, h].reshape(token_rows, width)).astype(jnp.bfloat16)
        sel_b[:, h] = chosen.reshape(ring, ranks * slots, width)
    ring_swap(1, sel_b, got_xb)
    wait_swap(1, got_xb)
    for h in range(2):
        mixed = exact_dot(turn, got_xb[:, h].reshape(slot_rows, width)).astype(jnp.bfloat16)
        blk_b[:, h] = mixed.reshape(ranks, chunk, width)
    send_deep(1, near, blk_b, rows_b.at[low(my_z, half)])
    wait_deep(0, all_z, lambda z: rows.at[chunk_of(z)])
    rows_x = rows[...].reshape(depth * chunk, width)
    weight_copies[0].wait()
    ring_send(0, exact_dot(rows_x, wg[...]))
    weight_copies[1].wait()
    ring_send(1, exact_dot(rows_x, wu[...]))
    wait_deep(1, near, lambda z: rows_b.at[low(z, half)])
    weight_copies[2].wait()
    back_part = exact_dot(rows_b[...].reshape(depth * chunk, width), wd[...])
    back_part = back_part.astype(jnp.bfloat16).reshape(ring, ranks, chunk, hidden)
    for r in range(ranks):
        part_zb[r] = back_part[:, r]
    for d in range(1, ranks):
        to = my_r ^ d
        go(remote(part_zb.at[to], got_zb.at[d], bz_send.at[d], bz_recv.at[d], at_z(z_base + to)))
    line_send(0)
    line_send(1)
    total = part_zb[my_r].astype(jnp.float32)
    for d in range(1, ranks):
        slot = got_zb.at[d]
        remote(slot, slot, bz_send.at[d], bz_recv.at[d], at_z(my_z)).wait_recv()
        total += got_zb[d].astype(jnp.float32)
    part_xb[...] = total.astype(jnp.bfloat16)
    for d in around:
        to = low(my_x + d, ring)
        go(remote(part_xb.at[to], got_rxb.at[d], bx_send.at[d], bx_recv.at[d], at_x(to)))
    gate = line_sum(0)
    up = line_sum(1)
    back = part_xb[my_x].astype(jnp.float32)
    for d in around:
        slot = got_rxb.at[d]
        remote(slot, slot, bx_send.at[d], bx_recv.at[d], at_x(my_x)).wait_recv()
        back += got_rxb[d].astype(jnp.float32)
    back *= row_p
    sig = 1.0 / (1.0 + jnp.exp(-gate))
    mine = my_x * ranks + my_r
    grads[mine, 0] = (back * up * sig * (1.0 + gate * (1.0 - sig))).astype(jnp.bfloat16)
    grads[mine, 1] = (back * gate * sig).astype(jnp.bfloat16)

    for j in range(1, ranks):
        go(remote(grads.at[mine], grads.at[mine], gz_send.at[j], gz_recv.at[j], at_z(z_base + (my_r ^ j))))
    for j in range(ranks):
        held = grads.at[my_x * ranks + (my_r ^ j)]
        if j:
            remote(held, held, gz_send.at[j], gz_recv.at[j], at_z(my_z)).wait_recv()
        for d in around:
            go(remote(held, held, gx_send.at[j, d], gx_recv.at[j, d], at_x(low(my_x + d, ring))))

    for d in [0] + around:
        owner = low(my_x - d, ring)
        first = owner * ranks
        if d:
            for j in range(ranks):
                slot = grads.at[first + (my_r ^ j)]
                remote(slot, slot, gx_send.at[j, d], gx_recv.at[j, d], at_x(my_x)).wait_recv()
        both = grads[pl.ds(first, ranks)]
        result = dot_nt(both[:, 0].reshape(ranks * chunk, hidden), wg[...])
        result += dot_nt(both[:, 1].reshape(ranks * chunk, hidden), wu[...])
        ret[pl.ds(first, ranks)] = result.astype(jnp.bfloat16).reshape(ranks, chunk, width)
        for j in range(ranks):
            at = first + j
            to = z_of(at)

            @pl.when(to != my_z)
            def _(at=at, to=to):
                remote(ret.at[at], got_ret.at[my_z], tz_send.at[to], tz_recv.at[my_z], at_z(to)).start()

    got_ret[my_z] = ret[chunk_of(my_z)]
    for d in range(1, depth):
        source = low(my_z - d, depth)
        slot = got_ret.at[source]
        remote(slot, slot, tz_send.at[source], tz_recv.at[source], at_z(my_z)).wait_recv()
    folded = exact_dot(fold, got_ret[...].reshape(blocks * slot_rows, width)).astype(jnp.bfloat16)
    ret_x[...] = folded.reshape(ring, ranks * slots, width)
    for d in range(1, ring):
        to = low(my_x + d, ring)
        go(remote(ret_x.at[to], got_retx.at[my_x], tx_send.at[d], tx_recv.at[d], at_x(to)))
    got_retx[my_x] = ret_x[my_x]
    for d in range(1, ring):
        slot = got_retx.at[low(my_x - d, ring)]
        remote(slot, slot, tx_send.at[d], tx_recv.at[d], at_x(my_x)).wait_recv()
    spread_rows = exact_dot(unpick, got_retx[...].reshape(slot_rows, width)).astype(jnp.bfloat16)
    scat[...] = spread_rows.reshape(groups, pieces, width)
    for d in range(1, groups):
        to = low(my_g + d, groups)
        go(remote(scat.at[low(to, 2) * lines + high(to, 2)], fin.at[d], tg_send.at[d], tg_recv.at[d], at_g(to)))
    total = scat[low(my_g, 2) * lines + high(my_g, 2)].astype(jnp.float32)
    for d in range(1, groups):
        slot = fin.at[d]
        remote(slot, slot, tg_send.at[d], tg_recv.at[d], at_g(my_g)).wait_recv()
        total += fin[d].astype(jnp.float32)
    out_ref[...] = total.astype(jnp.bfloat16)

    for copy in sent:
        copy.wait_send()
    for d in range(1, depth):
        to = low(my_z + d, depth)
        remote(ret.at[chunk_of(to)], got_ret.at[my_z], tz_send.at[to], tz_recv.at[my_z], at_z(to)).wait_send()


def run(sizes, tokens, routes, probs, w_gate, w_up, w_down):
    groups, blocks, ranks, ring, slots = sizes
    depth, pieces, chunk = blocks * ranks, ranks * ring, ring * slots
    width, hidden = w_gate.shape
    bf = jnp.bfloat16
    vmem = functools.partial(pltpu.VMEM, dtype=bf)
    dma = pltpu.SemaphoreType.DMA
    hbm_spec = pl.BlockSpec(memory_space=pltpu.HBM)
    vmem_spec = pl.BlockSpec(memory_space=pltpu.VMEM)
    return pl.pallas_call(
        functools.partial(kernel, sizes),
        out_shape=jax.ShapeDtypeStruct((pieces, width), bf),
        in_specs=[vmem_spec] + [hbm_spec] * 5,
        out_specs=vmem_spec,
        scratch_shapes=[
            pltpu.VMEM(routes.shape, routes.dtype),
            vmem(probs.shape),
            vmem((width, hidden)),
            vmem((width, hidden)),
            vmem((width, hidden)),
            vmem((2, pieces, width)),
            vmem((2, groups // 2, pieces, width)),
            vmem((2, groups // 2, 2, pieces, width)),
            vmem((ring, ranks * slots, width)),
            vmem((ring, 2, ranks * slots, width)),
            vmem((ring, ranks * slots, width)),
            vmem((ring, 2, ranks * slots, width)),
            vmem((ranks, chunk, width)),
            vmem((ranks, 2, chunk, width)),
            vmem((depth, chunk, width)),
            vmem((depth // 2, 2, chunk, width)),
            vmem((2, ring, ranks * chunk, hidden)),
            vmem((2, ring, ranks * chunk, hidden)),
            vmem((2, ranks, chunk, hidden)),
            vmem((2, ranks, chunk, hidden)),
            vmem((ranks, ring, chunk, hidden)),
            vmem((ranks, ring, chunk, hidden)),
            vmem((ring, chunk, hidden)),
            vmem((ring, chunk, hidden)),
            vmem((depth, 2, chunk, hidden)),
            vmem((depth, chunk, width)),
            vmem((depth, chunk, width)),
            vmem((ring, ranks * slots, width)),
            vmem((ring, ranks * slots, width)),
            vmem((groups, pieces, width)),
            vmem((groups, pieces, width)),
            dma((3,)),
            dma((2,)),
            dma(()),
            dma(()),
            dma((2, groups // 2)),
            dma((2, groups // 2)),
            dma((2,)),
            dma((2,)),
            dma((2, ring)),
            dma((2, ring)),
            dma((2, depth)),
            dma((2, depth)),
            dma((2, ring)),
            dma((2, ring)),
            dma((2, ranks)),
            dma((2, ranks)),
            dma((ranks,)),
            dma((ranks,)),
            dma((ring,)),
            dma((ring,)),
            dma((ranks,)),
            dma((ranks,)),
            dma((ranks, ring)),
            dma((ranks, ring)),
            dma((depth,)),
            dma((depth,)),
            dma((ring,)),
            dma((ring,)),
            dma((groups,)),
            dma((groups,)),
        ],
        compiler_params=pltpu.CompilerParams(
            collective_id=0, has_side_effects=True, vmem_limit_bytes=56 * 1024 * 1024
        ),
    )(tokens, routes, probs, w_gate, w_up, w_down)


def on_device(x_rows, grad_rows, routes, probs, w_gate, w_up, w_down, sizes):
    groups, blocks, ranks, ring, slots = sizes
    pieces, width = ranks * ring, w_gate.shape[1]
    tokens = jnp.stack([x_rows.reshape(pieces, width), grad_rows.reshape(pieces, width)])
    by_column = [jnp.swapaxes(array[:, :, 0], 1, 2) for array in (routes, probs)]
    result = run(sizes, tokens, *by_column, w_gate[0], w_up[0], jnp.swapaxes(w_down[0], 0, 1))
    return result.reshape(x_rows.shape)


def solution(mesh):
    sizes = (mesh.shape["group"], BLOCKS, RANKS, RING, SLOTS)
    in_specs = (
        P("group", "expert", None, None),
        P("group", "expert", None, None),
        P(),
        P(),
        P(("group", "expert"), None, None),
        P(("group", "expert"), None, None),
        P(("group", "expert"), None, None),
    )
    return jax.shard_map(
        functools.partial(on_device, sizes=sizes),
        mesh=mesh,
        in_specs=in_specs,
        out_specs=P("group", "expert", None, None),
        check_vma=False,
    )
```

```python
import functools

import jax
import jax.numpy as jnp
from jax import lax
from jax.experimental import pallas as pl
from jax.experimental.pallas import tpu as pltpu
from jax.sharding import PartitionSpec as P

MESH = pl.DeviceIdType.MESH
BLOCKS = 4
RANKS = 4
RING = 4
SLOTS = 4


def low(value, size):
    return value & (size - 1)


def high(value, size):
    return value >> (size.bit_length() - 1)


def onehot(mask):
    return jnp.where(mask, 1.0, 0.0).astype(jnp.bfloat16)


def exact_dot(left, right):
    return jnp.dot(left, right, preferred_element_type=jnp.float32)


def dot_nt(left, right):
    return lax.dot_general(left, right, (((1,), (1,)), ((), ())), preferred_element_type=jnp.float32)


def kernel(
    sizes,
    tok_ref,
    route_hbm,
    prob_hbm,
    wg_hbm,
    wu_hbm,
    wd_hbm,
    out_ref,
    route_ref,
    prob_ref,
    wg,
    wu,
    wd,
    pair,
    got_a,
    got_b,
    sel,
    sel_b,
    got_x,
    got_xb,
    blk,
    blk_b,
    rows,
    rows_b,
    part,
    got_rx,
    part_z,
    got_rz,
    part_zb,
    got_zb,
    part_xb,
    got_rxb,
    grads,
    ret,
    got_ret,
    ret_x,
    got_retx,
    scat,
    fin,
    w_sem,
    m_sem,
    p_send,
    p_recv,
    a_send,
    a_recv,
    c_send,
    c_recv,
    x_send,
    x_recv,
    z_send,
    z_recv,
    rx_send,
    rx_recv,
    rz_send,
    rz_recv,
    bz_send,
    bz_recv,
    bx_send,
    bx_recv,
    gz_send,
    gz_recv,
    gx_send,
    gx_recv,
    tz_send,
    tz_recv,
    tx_send,
    tx_recv,
    tg_send,
    tg_recv,
):
    groups, blocks, ranks, ring, slots = sizes
    depth = blocks * ranks
    pieces = ranks * ring
    chunk = ring * slots
    lines = groups // 2
    half = depth // 2
    width = tok_ref.shape[2]
    hidden = wg.shape[1] // 2
    my_g = lax.axis_index("group")
    my_e = lax.axis_index("expert")
    my_x = low(my_e, ring)
    my_z = high(my_e, ring)
    my_r = low(my_z, ranks)
    z_base = my_z - my_r
    my_core = low(my_g, 2)
    my_y = high(my_g, 2)
    my_half = high(my_z, half)

    def chunk_of(z):
        return low(z, half) * 2 + high(z, half)

    def z_of(at):
        return low(at, 2) * half + high(at, 2)

    def at_x(x):
        return (my_g, my_z * ring + x)

    def at_z(z):
        return (my_g, z * ring + my_x)

    def at_g(g):
        return (g, my_e)

    def remote(src, dst, send, recv, device):
        return pltpu.make_async_remote_copy(
            src_ref=src, dst_ref=dst, send_sem=send, recv_sem=recv, device_id=device, device_id_type=MESH
        )

    around = sorted(range(1, ring), key=lambda d: min(d, ring - d))
    sent = []

    def go(copy):
        copy.start()
        sent.append(copy)

    map_copies = [
        pltpu.make_async_copy(source, target, m_sem.at[at])
        for at, (source, target) in enumerate(((route_hbm, route_ref), (prob_hbm, prob_ref)))
    ]
    for copy in map_copies:
        copy.start()
    weight_copies = [
        pltpu.make_async_copy(source, target, w_sem.at[at])
        for at, (source, target) in enumerate(((wg_hbm, wg), (wu_hbm, wu), (wd_hbm, wd)))
    ]
    for copy in weight_copies:
        copy.start()

    barrier = pltpu.get_barrier_semaphore()
    for d in range(1, groups):
        pl.semaphore_signal(barrier, inc=1, device_id=at_g(low(my_g + d, groups)), device_id_type=MESH)
    for d in range(1, depth):
        pl.semaphore_signal(barrier, inc=1, device_id=at_z(low(my_z + d, depth)), device_id_type=MESH)
    for d in range(1, ring):
        pl.semaphore_signal(barrier, inc=1, device_id=at_x(low(my_x + d, ring)), device_id_type=MESH)

    slot_rows = ring * ranks * slots
    token_rows = groups * pieces

    for copy in map_copies:
        copy.wait()
    route = route_ref[...]
    columns = route.shape[2]
    in_group = jnp.max(jnp.where(high(route, blocks) == my_g, 1.0, 0.0), axis=1)
    expert = my_g * blocks + high(my_z, ranks)
    weight = jnp.sum(jnp.where(route == expert, prob_ref[...].astype(jnp.float32), 0.0), axis=1)
    lane = lax.broadcasted_iota(jnp.int32, (1, columns), 1)
    count = jnp.zeros((1, columns), jnp.float32)
    slot_token = [count] * slots
    slot_weight = [count] * slots
    for m in range(groups):
        named = in_group[m : m + 1]
        for s in range(slots):
            here = jnp.where(count == s, named, 0.0)
            slot_token[s] += here * (m % 2 * lines + m // 2)
            slot_weight[s] += here * weight[m : m + 1]
        count += named

    def tokens_of(column):
        return [
            jnp.sum(jnp.where(lane == column, token, 0.0), axis=1, keepdims=True).astype(jnp.int32)
            for token in slot_token
        ]

    my_tokens = tokens_of(my_e)
    pair_tokens = [tokens_of((h * half + low(my_z, half)) * ring + my_x) for h in range(2)]
    row = lax.broadcasted_iota(jnp.int32, (chunk, columns), 0)
    owned = z_of(my_x * ranks + my_r) * ring
    row_p = jnp.zeros((chunk, columns), jnp.float32)
    for s in range(slots):
        row_p = jnp.where(low(row, slots) == s, slot_weight[s], row_p)
    owner = owned + high(row, slots) == lax.broadcasted_iota(jnp.int32, (chunk, columns), 1)
    row_p = jnp.sum(jnp.where(owner, row_p, 0.0), axis=1, keepdims=True)

    def slot_of(index, tokens):
        s = low(index, slots)
        token = jnp.broadcast_to(tokens[0], index.shape)
        for at in range(1, slots):
            token = jnp.where(s == at, tokens[at], token)
        rest = high(index, slots)
        piece = low(rest, ranks) * ring + high(rest, ranks)
        return token * pieces + piece

    def picking(tokens):
        shape = (slot_rows, token_rows)
        return onehot(
            slot_of(lax.broadcasted_iota(jnp.int32, shape, 0), tokens)
            == lax.broadcasted_iota(jnp.int32, shape, 1)
        )

    shape = (token_rows, slot_rows)
    unpick = onehot(
        slot_of(lax.broadcasted_iota(jnp.int32, shape, 1), my_tokens)
        == lax.broadcasted_iota(jnp.int32, shape, 0)
    )
    picks = [picking(my_tokens)] + [picking(tokens) for tokens in pair_tokens]
    shape = (slot_rows, slot_rows)
    row = lax.broadcasted_iota(jnp.int32, shape, 0)
    rest = high(row, slots)
    turned = (low(rest, ring) * ranks + high(rest, ring)) * slots + low(row, slots)
    turn = onehot(lax.broadcasted_iota(jnp.int32, shape, 1) == turned)
    shape = (slot_rows, blocks * slot_rows)
    row = lax.broadcasted_iota(jnp.int32, shape, 0)
    rest = high(row, slots)
    turned = (low(rest, ranks) * ring + high(rest, ranks)) * slots + low(row, slots)
    fold = onehot(low(lax.broadcasted_iota(jnp.int32, shape, 1), slot_rows) == turned)

    pl.semaphore_wait(barrier, groups + depth + ring - 3)

    far_first = sorted(range(1, lines), key=lambda d: -min(d, lines - d))

    def spread(a, source, target):
        for d in far_first:
            to = low(my_y + d, lines) * 2 + my_core
            go(remote(source, target.at[my_core, my_y], a_send.at[a, d], a_recv.at[a, d], at_g(to)))
        target[my_core, my_y] = source[...]

    def share(a, target):
        for d in range(1, lines):
            slot = target.at[my_core, low(my_y - d, lines)]
            remote(slot, slot, a_send.at[a, d], a_recv.at[a, d], at_g(my_g)).wait_recv()
        mine = target.at[my_core]
        go(remote(mine, mine, c_send.at[a], c_recv.at[a], at_g(my_y * 2 + 1 - my_core)))

    def wait_share(a, target):
        slot = target.at[1 - my_core]
        remote(slot, slot, c_send.at[a], c_recv.at[a], at_g(my_g)).wait_recv()

    def ring_swap(a, source, target):
        for d in range(1, ring):
            to = low(my_x + d, ring)
            go(remote(source.at[to], target.at[my_x], x_send.at[a, d], x_recv.at[a, d], at_x(to)))
        target[my_x] = source[my_x]

    def wait_swap(a, target):
        for d in range(1, ring):
            slot = target.at[low(my_x - d, ring)]
            remote(slot, slot, x_send.at[a, d], x_recv.at[a, d], at_x(my_x)).wait_recv()

    near = list(range(1, depth // 4 + 1)) + list(range(depth - depth // 4 + 1, depth))
    near.sort(key=lambda d: min(d, depth - d))
    all_z = sorted(range(1, depth), key=lambda d: min(d, depth - d))

    way = 1 - 2 * my_core

    def send_deep(a, steps, source, slot):
        for d in steps:
            to = low(my_z + way * d, depth)
            go(remote(source.at[low(to, ranks)], slot, z_send.at[a, d], z_recv.at[a, d], at_z(to)))
        slot[...] = source[my_r]

    def wait_deep(a, steps, slot_from):
        for d in steps:
            slot = slot_from(low(my_z - way * d, depth))
            remote(slot, slot, z_send.at[a, d], z_recv.at[a, d], at_z(my_z)).wait_recv()

    def half_of(weight, h):
        return weight[:, h * hidden : (h + 1) * hidden]

    def ring_send(q, h, value):
        part[q, h] = value.astype(jnp.bfloat16).reshape(ring, ranks * chunk, hidden)
        for d in around:
            to = low(my_x + d, ring)
            go(remote(part.at[q, h, to], got_rx.at[q, h, d], rx_send.at[q, h, d], rx_recv.at[q, h, d], at_x(to)))

    def line_send(q, h):
        total = part[q, h, my_x].astype(jnp.float32)
        for d in around:
            slot = got_rx.at[q, h, d]
            remote(slot, slot, rx_send.at[q, h, d], rx_recv.at[q, h, d], at_x(my_x)).wait_recv()
            total += got_rx[q, h, d].astype(jnp.float32)
        part_z[q, h] = total.astype(jnp.bfloat16).reshape(ranks, chunk, hidden)
        for d in range(1, ranks):
            to = my_r ^ d
            device = at_z(z_base + to)
            go(remote(part_z.at[q, h, to], got_rz.at[q, h, d], rz_send.at[q, h, d], rz_recv.at[q, h, d], device))

    def line_sum(q, h):
        total = part_z[q, h, my_r].astype(jnp.float32)
        for d in range(1, ranks):
            slot = got_rz.at[q, h, d]
            remote(slot, slot, rz_send.at[q, h, d], rz_recv.at[q, h, d], at_z(my_z)).wait_recv()
            total += got_rz[q, h, d].astype(jnp.float32)
        return total

    mine = my_x * ranks + my_r

    def activate(h, back):
        gate = line_sum(0, h)
        up = line_sum(1, h)
        back = back() * row_p
        sig = 1.0 / (1.0 + jnp.exp(-gate))
        grads[h, mine, 0] = (back * up * sig * (1.0 + gate * (1.0 - sig))).astype(jnp.bfloat16)
        grads[h, mine, 1] = (back * gate * sig).astype(jnp.bfloat16)
        held = grads.at[h, mine]
        for j in range(1, ranks):
            go(remote(held, held, gz_send.at[h, j], gz_recv.at[h, j], at_z(z_base + (my_r ^ j))))
        pass_on(h, 0)

    def pass_on(h, j):
        held = grads.at[h, my_x * ranks + (my_r ^ j)]
        if j:
            remote(held, held, gz_send.at[h, j], gz_recv.at[h, j], at_z(my_z)).wait_recv()
        for d in around:
            go(remote(held, held, gx_send.at[h, j, d], gx_recv.at[h, j, d], at_x(low(my_x + d, ring))))

    spread(0, tok_ref.at[0], got_a)
    go(remote(tok_ref.at[1], pair.at[my_half], p_send, p_recv, at_z(low(my_z + half, depth))))
    pair[my_half] = tok_ref[1]
    share(0, got_a)
    slot = pair.at[1 - my_half]
    remote(slot, slot, p_send, p_recv, at_z(my_z)).wait_recv()
    spread(1, pair, got_b)
    wait_share(0, got_a)
    chosen = exact_dot(picks[0], got_a[...].reshape(token_rows, width)).astype(jnp.bfloat16)
    sel[...] = chosen.reshape(ring, ranks * slots, width)
    ring_swap(0, sel, got_x)
    wait_swap(0, got_x)
    mixed = exact_dot(turn, got_x[...].reshape(slot_rows, width)).astype(jnp.bfloat16)
    blk[...] = mixed.reshape(ranks, chunk, width)
    send_deep(0, all_z, blk, rows.at[chunk_of(my_z)])
    share(1, got_b)
    wait_share(1, got_b)
    for h in range(2):
        chosen = exact_dot(picks[1 + h], got_b[:, :, h].reshape(token_rows, width)).astype(jnp.bfloat16)
        sel_b[:, h] = chosen.reshape(ring, ranks * slots, width)
    ring_swap(1, sel_b, got_xb)
    wait_swap(1, got_xb)
    for h in range(2):
        mixed = exact_dot(turn, got_xb[:, h].reshape(slot_rows, width)).astype(jnp.bfloat16)
        blk_b[:, h] = mixed.reshape(ranks, chunk, width)
    send_deep(1, near, blk_b, rows_b.at[low(my_z, half)])
    wait_deep(0, all_z, lambda z: rows.at[chunk_of(z)])
    rows_x = rows[...].reshape(depth * chunk, width)
    weight_copies[0].wait()
    weight_copies[1].wait()
    for h in range(2):
        ring_send(0, h, exact_dot(rows_x, half_of(wg, h)))
        ring_send(1, h, exact_dot(rows_x, half_of(wu, h)))
    wait_deep(1, near, lambda z: rows_b.at[low(z, half)])
    weight_copies[2].wait()
    rows_g = rows_b[...].reshape(depth * chunk, width)
    back_part = exact_dot(rows_g, half_of(wd, 0)).astype(jnp.bfloat16).reshape(ring, ranks, chunk, hidden)
    for r in range(ranks):
        part_zb[r] = back_part[:, r]
    for d in range(1, ranks):
        to = my_r ^ d
        go(remote(part_zb.at[to], got_zb.at[d], bz_send.at[d], bz_recv.at[d], at_z(z_base + to)))
    ring_send(2, 1, exact_dot(rows_g, half_of(wd, 1)))
    line_send(0, 0)
    line_send(1, 0)
    total = part_zb[my_r].astype(jnp.float32)
    for d in range(1, ranks):
        slot = got_zb.at[d]
        remote(slot, slot, bz_send.at[d], bz_recv.at[d], at_z(my_z)).wait_recv()
        total += got_zb[d].astype(jnp.float32)
    part_xb[...] = total.astype(jnp.bfloat16)
    for d in around:
        to = low(my_x + d, ring)
        go(remote(part_xb.at[to], got_rxb.at[d], bx_send.at[d], bx_recv.at[d], at_x(to)))
    line_send(0, 1)
    line_send(1, 1)
    line_send(2, 1)

    def back_first():
        back = part_xb[my_x].astype(jnp.float32)
        for d in around:
            slot = got_rxb.at[d]
            remote(slot, slot, bx_send.at[d], bx_recv.at[d], at_x(my_x)).wait_recv()
            back += got_rxb[d].astype(jnp.float32)
        return back

    activate(0, back_first)
    activate(1, lambda: line_sum(2, 1))
    for h in range(2):
        for j in range(1, ranks):
            pass_on(h, j)

    for d in [0] + around:
        owner = low(my_x - d, ring)
        first = owner * ranks
        if d:
            for h in range(2):
                for j in range(ranks):
                    slot = grads.at[h, first + (my_r ^ j)]
                    remote(slot, slot, gx_send.at[h, j, d], gx_recv.at[h, j, d], at_x(my_x)).wait_recv()
        result = jnp.zeros((ranks * chunk, width), jnp.float32)
        for h in range(2):
            both = grads[h, pl.ds(first, ranks)]
            for q, weight in enumerate((wg, wu)):
                result += dot_nt(both[:, q].reshape(ranks * chunk, hidden), half_of(weight, h))
        ret[pl.ds(first, ranks)] = result.astype(jnp.bfloat16).reshape(ranks, chunk, width)
        for j in range(ranks):
            at = first + j
            to = z_of(at)

            @pl.when(to != my_z)
            def _(at=at, to=to):
                remote(ret.at[at], got_ret.at[my_z], tz_send.at[to], tz_recv.at[my_z], at_z(to)).start()

    got_ret[my_z] = ret[chunk_of(my_z)]
    for d in range(1, depth):
        source = low(my_z - d, depth)
        slot = got_ret.at[source]
        remote(slot, slot, tz_send.at[source], tz_recv.at[source], at_z(my_z)).wait_recv()
    folded = exact_dot(fold, got_ret[...].reshape(blocks * slot_rows, width)).astype(jnp.bfloat16)
    ret_x[...] = folded.reshape(ring, ranks * slots, width)
    for d in range(1, ring):
        to = low(my_x + d, ring)
        go(remote(ret_x.at[to], got_retx.at[my_x], tx_send.at[d], tx_recv.at[d], at_x(to)))
    got_retx[my_x] = ret_x[my_x]
    for d in range(1, ring):
        slot = got_retx.at[low(my_x - d, ring)]
        remote(slot, slot, tx_send.at[d], tx_recv.at[d], at_x(my_x)).wait_recv()
    spread_rows = exact_dot(unpick, got_retx[...].reshape(slot_rows, width)).astype(jnp.bfloat16)
    scat[...] = spread_rows.reshape(groups, pieces, width)
    for d in range(1, groups):
        to = low(my_g + d, groups)
        go(remote(scat.at[low(to, 2) * lines + high(to, 2)], fin.at[d], tg_send.at[d], tg_recv.at[d], at_g(to)))
    total = scat[low(my_g, 2) * lines + high(my_g, 2)].astype(jnp.float32)
    for d in range(1, groups):
        slot = fin.at[d]
        remote(slot, slot, tg_send.at[d], tg_recv.at[d], at_g(my_g)).wait_recv()
        total += fin[d].astype(jnp.float32)
    out_ref[...] = total.astype(jnp.bfloat16)

    for copy in sent:
        copy.wait_send()
    for d in range(1, depth):
        to = low(my_z + d, depth)
        remote(ret.at[chunk_of(to)], got_ret.at[my_z], tz_send.at[to], tz_recv.at[my_z], at_z(to)).wait_send()


def run(sizes, tokens, routes, probs, w_gate, w_up, w_down):
    groups, blocks, ranks, ring, slots = sizes
    depth, pieces, chunk = blocks * ranks, ranks * ring, ring * slots
    width, hidden = w_gate.shape
    part = hidden // 2
    bf = jnp.bfloat16
    vmem = functools.partial(pltpu.VMEM, dtype=bf)
    dma = pltpu.SemaphoreType.DMA
    hbm_spec = pl.BlockSpec(memory_space=pltpu.HBM)
    vmem_spec = pl.BlockSpec(memory_space=pltpu.VMEM)
    return pl.pallas_call(
        functools.partial(kernel, sizes),
        out_shape=jax.ShapeDtypeStruct((pieces, width), bf),
        in_specs=[vmem_spec] + [hbm_spec] * 5,
        out_specs=vmem_spec,
        scratch_shapes=[
            pltpu.VMEM(routes.shape, routes.dtype),
            vmem(probs.shape),
            vmem((width, hidden)),
            vmem((width, hidden)),
            vmem((width, hidden)),
            vmem((2, pieces, width)),
            vmem((2, groups // 2, pieces, width)),
            vmem((2, groups // 2, 2, pieces, width)),
            vmem((ring, ranks * slots, width)),
            vmem((ring, 2, ranks * slots, width)),
            vmem((ring, ranks * slots, width)),
            vmem((ring, 2, ranks * slots, width)),
            vmem((ranks, chunk, width)),
            vmem((ranks, 2, chunk, width)),
            vmem((depth, chunk, width)),
            vmem((depth // 2, 2, chunk, width)),
            vmem((3, 2, ring, ranks * chunk, part)),
            vmem((3, 2, ring, ranks * chunk, part)),
            vmem((3, 2, ranks, chunk, part)),
            vmem((3, 2, ranks, chunk, part)),
            vmem((ranks, ring, chunk, part)),
            vmem((ranks, ring, chunk, part)),
            vmem((ring, chunk, part)),
            vmem((ring, chunk, part)),
            vmem((2, depth, 2, chunk, part)),
            vmem((depth, chunk, width)),
            vmem((depth, chunk, width)),
            vmem((ring, ranks * slots, width)),
            vmem((ring, ranks * slots, width)),
            vmem((groups, pieces, width)),
            vmem((groups, pieces, width)),
            dma((3,)),
            dma((2,)),
            dma(()),
            dma(()),
            dma((2, groups // 2)),
            dma((2, groups // 2)),
            dma((2,)),
            dma((2,)),
            dma((2, ring)),
            dma((2, ring)),
            dma((2, depth)),
            dma((2, depth)),
            dma((3, 2, ring)),
            dma((3, 2, ring)),
            dma((3, 2, ranks)),
            dma((3, 2, ranks)),
            dma((ranks,)),
            dma((ranks,)),
            dma((ring,)),
            dma((ring,)),
            dma((2, ranks)),
            dma((2, ranks)),
            dma((2, ranks, ring)),
            dma((2, ranks, ring)),
            dma((depth,)),
            dma((depth,)),
            dma((ring,)),
            dma((ring,)),
            dma((groups,)),
            dma((groups,)),
        ],
        compiler_params=pltpu.CompilerParams(
            collective_id=0, has_side_effects=True, vmem_limit_bytes=32 * 1024 * 1024
        ),
    )(tokens, routes, probs, w_gate, w_up, w_down)


def on_device(x_rows, grad_rows, routes, probs, w_gate, w_up, w_down, sizes):
    groups, blocks, ranks, ring, slots = sizes
    pieces, width = ranks * ring, w_gate.shape[1]
    tokens = jnp.stack([x_rows.reshape(pieces, width), grad_rows.reshape(pieces, width)])
    by_column = [jnp.swapaxes(array[:, :, 0], 1, 2) for array in (routes, probs)]
    result = run(sizes, tokens, *by_column, w_gate[0], w_up[0], jnp.swapaxes(w_down[0], 0, 1))
    return result.reshape(x_rows.shape)


def solution(mesh):
    sizes = (mesh.shape["group"], BLOCKS, RANKS, RING, SLOTS)
    in_specs = (
        P("group", "expert", None, None),
        P("group", "expert", None, None),
        P(),
        P(),
        P(("group", "expert"), None, None),
        P(("group", "expert"), None, None),
        P(("group", "expert"), None, None),
    )
    return jax.shard_map(
        functools.partial(on_device, sizes=sizes),
        mesh=mesh,
        in_specs=in_specs,
        out_specs=P("group", "expert", None, None),
        check_vma=False,
    )
```

```python
import functools

import jax
import jax.numpy as jnp
from jax import lax
from jax.experimental import pallas as pl
from jax.experimental.pallas import tpu as pltpu
from jax.sharding import PartitionSpec as P

MESH = pl.DeviceIdType.MESH
BLOCKS = 4
RANKS = 4
RING = 4
SLOTS = 4


def low(value, size):
    return value & (size - 1)


def high(value, size):
    return value >> (size.bit_length() - 1)


def onehot(mask):
    return jnp.where(mask, 1.0, 0.0).astype(jnp.bfloat16)


def exact_dot(left, right):
    return jnp.dot(left, right, preferred_element_type=jnp.float32)


def dot_nt(left, right):
    return lax.dot_general(left, right, (((1,), (1,)), ((), ())), preferred_element_type=jnp.float32)


def kernel(
    sizes,
    tok_ref,
    route_hbm,
    prob_hbm,
    wg_hbm,
    wu_hbm,
    wd_hbm,
    out_ref,
    route_ref,
    prob_ref,
    wg,
    wu,
    wd,
    tok,
    landed,
    pair,
    got_a,
    got_b,
    blk,
    blk_b,
    rows,
    rows_b,
    part,
    got_rx,
    part_z,
    got_rz,
    part_zb,
    got_zb,
    part_xb,
    got_rxb,
    grads,
    ret,
    got_ret,
    scat,
    fin,
    w_sem,
    m_sem,
    p_send,
    p_recv,
    a_send,
    a_recv,
    c_send,
    c_recv,
    z_send,
    z_recv,
    rx_send,
    rx_recv,
    rz_send,
    rz_recv,
    bz_send,
    bz_recv,
    bx_send,
    bx_recv,
    gz_send,
    gz_recv,
    gx_send,
    gx_recv,
    tz_send,
    tz_recv,
    tg_send,
    tg_recv,
):
    groups, blocks, ranks, ring, slots = sizes
    depth = blocks * ranks
    pieces = ranks * ring
    chunk = ring * slots
    lines = groups // 2
    half = depth // 2
    width = tok_ref.shape[2]
    hidden = wg.shape[1] // 2
    my_g = lax.axis_index("group")
    my_e = lax.axis_index("expert")
    my_x = low(my_e, ring)
    my_z = high(my_e, ring)
    my_r = low(my_z, ranks)
    z_base = my_z - my_r
    my_core = low(my_g, 2)
    my_y = high(my_g, 2)
    my_half = high(my_z, half)

    def chunk_of(z):
        return low(z, half) * 2 + high(z, half)

    def z_of(at):
        return low(at, 2) * half + high(at, 2)

    def at_x(x):
        return (my_g, my_z * ring + x)

    def at_z(z):
        return (my_g, z * ring + my_x)

    def at_g(g):
        return (g, my_e)

    def at_gx(g, x):
        return (g, my_z * ring + x)

    def remote(src, dst, send, recv, device):
        return pltpu.make_async_remote_copy(
            src_ref=src, dst_ref=dst, send_sem=send, recv_sem=recv, device_id=device, device_id_type=MESH
        )

    around = sorted(range(1, ring), key=lambda d: min(d, ring - d))
    sent = []

    def go(copy):
        copy.start()
        sent.append(copy)

    map_copies = [
        pltpu.make_async_copy(source, target, m_sem.at[at])
        for at, (source, target) in enumerate(((route_hbm, route_ref), (prob_hbm, prob_ref)))
    ]
    for copy in map_copies:
        copy.start()
    weight_copies = [
        pltpu.make_async_copy(source, target, w_sem.at[at])
        for at, (source, target) in enumerate(((wg_hbm, wg), (wu_hbm, wu), (wd_hbm, wd)))
    ]
    for copy in weight_copies:
        copy.start()

    barrier = pltpu.get_barrier_semaphore()
    column = [(dg, dx) for dg in range(groups) for dx in range(ring) if dg or dx]
    for dg, dx in column:
        device = at_gx(low(my_g + dg, groups), low(my_x + dx, ring))
        pl.semaphore_signal(barrier, inc=1, device_id=device, device_id_type=MESH)
    for d in range(1, depth):
        pl.semaphore_signal(barrier, inc=1, device_id=at_z(low(my_z + d, depth)), device_id_type=MESH)

    shape = (pieces, pieces)
    row = lax.broadcasted_iota(jnp.int32, shape, 0)
    by_x = onehot(lax.broadcasted_iota(jnp.int32, shape, 1) == low(row, ranks) * ring + high(row, ranks))
    for a in range(2):
        tok[a] = exact_dot(by_x, tok_ref[a]).astype(jnp.bfloat16).reshape(ring, ranks, width)
    pl.semaphore_wait(barrier, groups * ring - 1 + depth - 1)

    steps = [(dy, dx) for dy in range(lines) for dx in range(ring) if dy or dx]
    steps.sort(key=lambda step: -min(step[0], lines - step[0]) - min(step[1], ring - step[1]))

    def spread(a, source, target):
        for dy, dx in steps:
            y, x = low(my_y + dy, lines), low(my_x + dx, ring)
            device = at_gx(y * 2 + my_core, x)
            go(remote(source.at[x], target.at[my_core, my_y, my_x], a_send.at[a, dy, dx], a_recv.at[a, dy, dx], device))
        target[my_core, my_y, my_x] = source[my_x]

    def share(a, target):
        for dy, dx in steps:
            slot = target.at[my_core, low(my_y - dy, lines), low(my_x - dx, ring)]
            remote(slot, slot, a_send.at[a, dy, dx], a_recv.at[a, dy, dx], at_g(my_g)).wait_recv()
        mine = target.at[my_core]
        go(remote(mine, mine, c_send.at[a], c_recv.at[a], at_g(my_y * 2 + 1 - my_core)))

    def wait_share(a, target):
        slot = target.at[1 - my_core]
        remote(slot, slot, c_send.at[a], c_recv.at[a], at_g(my_g)).wait_recv()

    spread(0, tok.at[0], got_a)
    go(remote(tok.at[1], landed, p_send, p_recv, at_z(low(my_z + half, depth))))
    slot_rows = ring * ranks * slots
    token_rows = groups * pieces

    for copy in map_copies:
        copy.wait()
    route = route_ref[...]
    columns = route.shape[2]
    in_group = jnp.max(jnp.where(high(route, blocks) == my_g, 1.0, 0.0), axis=1)
    expert = my_g * blocks + high(my_z, ranks)
    weight = jnp.sum(jnp.where(route == expert, prob_ref[...].astype(jnp.float32), 0.0), axis=1)
    count = jnp.zeros((1, columns), jnp.float32)
    slot_token = [count] * slots
    slot_weight = [count] * slots
    for m in range(groups):
        named = in_group[m : m + 1]
        for s in range(slots):
            here = jnp.where(count == s, named, 0.0)
            slot_token[s] += here * (m % 2 * lines + m // 2)
            slot_weight[s] += here * weight[m : m + 1]
        count += named
    row = lax.broadcasted_iota(jnp.int32, (chunk, columns), 0)
    owned = z_of(my_x * ranks + my_r) * ring
    row_p = jnp.zeros((chunk, columns), jnp.float32)
    for s in range(slots):
        row_p = jnp.where(low(row, slots) == s, slot_weight[s], row_p)
    owner = owned + high(row, slots) == lax.broadcasted_iota(jnp.int32, (chunk, columns), 1)
    row_p = jnp.sum(jnp.where(owner, row_p, 0.0), axis=1, keepdims=True)

    def picking(z):
        row = lax.broadcasted_iota(jnp.int32, (slot_rows, columns), 0)
        token = jnp.zeros((slot_rows, columns), jnp.float32)
        for s in range(slots):
            token = jnp.where(low(row, slots) == s, slot_token[s], token)
        at = z * ring + low(high(row, slots), ring)
        token = jnp.where(lax.broadcasted_iota(jnp.int32, (slot_rows, columns), 1) == at, token, 0.0)
        token = jnp.sum(token, axis=1, keepdims=True).astype(jnp.int32)
        row = lax.broadcasted_iota(jnp.int32, (slot_rows, 1), 0)
        rest = high(row, slots)
        wanted = (token * ring + low(rest, ring)) * ranks + high(rest, ring)
        return onehot(wanted == lax.broadcasted_iota(jnp.int32, (slot_rows, token_rows), 1))

    pick = picking(my_z)
    pick_pair = [picking(h * half + low(my_z, half)) for h in range(2)]

    near = list(range(1, depth // 4 + 1)) + list(range(depth - depth // 4 + 1, depth))
    near.sort(key=lambda d: min(d, depth - d))
    all_z = sorted(range(1, depth), key=lambda d: min(d, depth - d))

    way = 1 - 2 * my_core

    def send_deep(a, steps, source, slot):
        for d in steps:
            to = low(my_z + way * d, depth)
            go(remote(source.at[low(to, ranks)], slot, z_send.at[a, d], z_recv.at[a, d], at_z(to)))
        slot[...] = source[my_r]

    def wait_deep(a, steps, slot_from):
        for d in steps:
            slot = slot_from(low(my_z - way * d, depth))
            remote(slot, slot, z_send.at[a, d], z_recv.at[a, d], at_z(my_z)).wait_recv()

    def half_of(weight, h):
        return weight[:, h * hidden : (h + 1) * hidden]

    def ring_send(q, h, value):
        part[q, h] = value.astype(jnp.bfloat16).reshape(ring, ranks * chunk, hidden)
        for d in around:
            to = low(my_x + d, ring)
            go(remote(part.at[q, h, to], got_rx.at[q, h, d], rx_send.at[q, h, d], rx_recv.at[q, h, d], at_x(to)))

    def line_send(q, h):
        total = part[q, h, my_x].astype(jnp.float32)
        for d in around:
            slot = got_rx.at[q, h, d]
            remote(slot, slot, rx_send.at[q, h, d], rx_recv.at[q, h, d], at_x(my_x)).wait_recv()
            total += got_rx[q, h, d].astype(jnp.float32)
        part_z[q, h] = total.astype(jnp.bfloat16).reshape(ranks, chunk, hidden)
        for d in range(1, ranks):
            to = my_r ^ d
            device = at_z(z_base + to)
            go(remote(part_z.at[q, h, to], got_rz.at[q, h, d], rz_send.at[q, h, d], rz_recv.at[q, h, d], device))

    def line_sum(q, h):
        total = part_z[q, h, my_r].astype(jnp.float32)
        for d in range(1, ranks):
            slot = got_rz.at[q, h, d]
            remote(slot, slot, rz_send.at[q, h, d], rz_recv.at[q, h, d], at_z(my_z)).wait_recv()
            total += got_rz[q, h, d].astype(jnp.float32)
        return total

    mine = my_x * ranks + my_r

    def activate(h, back):
        gate = line_sum(0, h)
        up = line_sum(1, h)
        back = back() * row_p
        sig = 1.0 / (1.0 + jnp.exp(-gate))
        grads[h, mine, 0] = (back * up * sig * (1.0 + gate * (1.0 - sig))).astype(jnp.bfloat16)
        grads[h, mine, 1] = (back * gate * sig).astype(jnp.bfloat16)
        held = grads.at[h, mine]
        for j in range(1, ranks):
            go(remote(held, held, gz_send.at[h, j], gz_recv.at[h, j], at_z(z_base + (my_r ^ j))))
        pass_on(h, 0)

    def pass_on(h, j):
        held = grads.at[h, my_x * ranks + (my_r ^ j)]
        if j:
            remote(held, held, gz_send.at[h, j], gz_recv.at[h, j], at_z(my_z)).wait_recv()
        for d in around:
            go(remote(held, held, gx_send.at[h, j, d], gx_recv.at[h, j, d], at_x(low(my_x + d, ring))))

    share(0, got_a)
    remote(landed, landed, p_send, p_recv, at_z(my_z)).wait_recv()
    pair[:, my_half] = tok[1]
    pair[:, 1 - my_half] = landed[...]
    spread(1, pair, got_b)
    wait_share(0, got_a)
    chosen = exact_dot(pick, got_a[...].reshape(token_rows, width)).astype(jnp.bfloat16)
    blk[...] = chosen.reshape(ranks, chunk, width)
    send_deep(0, all_z, blk, rows.at[chunk_of(my_z)])
    share(1, got_b)
    wait_share(1, got_b)
    for h in range(2):
        chosen = exact_dot(pick_pair[h], got_b[:, :, :, h].reshape(token_rows, width)).astype(jnp.bfloat16)
        blk_b[:, h] = chosen.reshape(ranks, chunk, width)
    send_deep(1, near, blk_b, rows_b.at[low(my_z, half)])
    wait_deep(0, all_z, lambda z: rows.at[chunk_of(z)])
    rows_x = rows[...].reshape(depth * chunk, width)
    weight_copies[0].wait()
    weight_copies[1].wait()
    for h in range(2):
        ring_send(0, h, exact_dot(rows_x, half_of(wg, h)))
        ring_send(1, h, exact_dot(rows_x, half_of(wu, h)))
    wait_deep(1, near, lambda z: rows_b.at[low(z, half)])
    weight_copies[2].wait()
    rows_g = rows_b[...].reshape(depth * chunk, width)
    back_part = exact_dot(rows_g, half_of(wd, 0)).astype(jnp.bfloat16).reshape(ring, ranks, chunk, hidden)
    for r in range(ranks):
        part_zb[r] = back_part[:, r]
    for d in range(1, ranks):
        to = my_r ^ d
        go(remote(part_zb.at[to], got_zb.at[d], bz_send.at[d], bz_recv.at[d], at_z(z_base + to)))
    ring_send(2, 1, exact_dot(rows_g, half_of(wd, 1)))
    line_send(0, 0)
    line_send(1, 0)
    total = part_zb[my_r].astype(jnp.float32)
    for d in range(1, ranks):
        slot = got_zb.at[d]
        remote(slot, slot, bz_send.at[d], bz_recv.at[d], at_z(my_z)).wait_recv()
        total += got_zb[d].astype(jnp.float32)
    part_xb[...] = total.astype(jnp.bfloat16)
    for d in around:
        to = low(my_x + d, ring)
        go(remote(part_xb.at[to], got_rxb.at[d], bx_send.at[d], bx_recv.at[d], at_x(to)))
    line_send(0, 1)
    line_send(1, 1)
    line_send(2, 1)

    def back_first():
        back = part_xb[my_x].astype(jnp.float32)
        for d in around:
            slot = got_rxb.at[d]
            remote(slot, slot, bx_send.at[d], bx_recv.at[d], at_x(my_x)).wait_recv()
            back += got_rxb[d].astype(jnp.float32)
        return back

    activate(0, back_first)
    activate(1, lambda: line_sum(2, 1))
    for h in range(2):
        for j in range(1, ranks):
            pass_on(h, j)

    for d in [0] + around:
        owner = low(my_x - d, ring)
        first = owner * ranks
        if d:
            for h in range(2):
                for j in range(ranks):
                    slot = grads.at[h, first + (my_r ^ j)]
                    remote(slot, slot, gx_send.at[h, j, d], gx_recv.at[h, j, d], at_x(my_x)).wait_recv()
        result = jnp.zeros((ranks * chunk, width), jnp.float32)
        for h in range(2):
            both = grads[h, pl.ds(first, ranks)]
            for q, weight in enumerate((wg, wu)):
                result += dot_nt(both[:, q].reshape(ranks * chunk, hidden), half_of(weight, h))
        ret[pl.ds(first, ranks)] = result.astype(jnp.bfloat16).reshape(ranks, chunk, width)
        for j in range(ranks):
            at = first + j
            to = z_of(at)

            @pl.when(to != my_z)
            def _(at=at, to=to):
                remote(ret.at[at], got_ret.at[my_z], tz_send.at[to], tz_recv.at[my_z], at_z(to)).start()

    got_ret[my_z] = ret[chunk_of(my_z)]
    for d in range(1, depth):
        source = low(my_z - d, depth)
        slot = got_ret.at[source]
        remote(slot, slot, tz_send.at[source], tz_recv.at[source], at_z(my_z)).wait_recv()
    folded = got_ret[:ranks].astype(jnp.float32)
    for block in range(1, blocks):
        folded += got_ret[block * ranks : (block + 1) * ranks].astype(jnp.float32)
    folded = folded.astype(jnp.bfloat16).reshape(slot_rows, width)
    scattered = lax.dot_general(pick, folded, (((0,), (0,)), ((), ())), preferred_element_type=jnp.float32)
    scat[...] = scattered.astype(jnp.bfloat16).reshape(groups, ring, ranks, width)

    def place(g):
        return low(g, 2) * lines + high(g, 2)

    def hops(step):
        dy = step[0] // 2
        return min(dy, lines - dy) + min(step[1], ring - step[1])

    column.sort(key=lambda step: -hops(step))
    for dg, dx in column:
        g, x = low(my_g + dg, groups), low(my_x + dx, ring)
        go(remote(scat.at[place(g), x], fin.at[my_x, dg], tg_send.at[dg, dx], tg_recv.at[dg, dx], at_gx(g, x)))
    fin[my_x, 0] = scat[place(my_g), my_x]
    shape = (pieces, token_rows)
    row = lax.broadcasted_iota(jnp.int32, shape, 0)
    col = lax.broadcasted_iota(jnp.int32, shape, 1)
    same_x = high(high(col, ranks), groups) == low(row, ring)
    gather = onehot(same_x & (low(col, ranks) == high(row, ring)))
    for dg, dx in column:
        slot = fin.at[low(my_x - dx, ring), dg]
        remote(slot, slot, tg_send.at[dg, dx], tg_recv.at[dg, dx], at_g(my_g)).wait_recv()
    out_ref[...] = exact_dot(gather, fin[...].reshape(token_rows, width)).astype(jnp.bfloat16)

    for copy in sent:
        copy.wait_send()
    for d in range(1, depth):
        to = low(my_z + d, depth)
        remote(ret.at[chunk_of(to)], got_ret.at[my_z], tz_send.at[to], tz_recv.at[my_z], at_z(to)).wait_send()


def run(sizes, tokens, routes, probs, w_gate, w_up, w_down):
    groups, blocks, ranks, ring, slots = sizes
    depth, pieces, chunk = blocks * ranks, ranks * ring, ring * slots
    width, hidden = w_gate.shape
    part = hidden // 2
    bf = jnp.bfloat16
    vmem = functools.partial(pltpu.VMEM, dtype=bf)
    dma = pltpu.SemaphoreType.DMA
    hbm_spec = pl.BlockSpec(memory_space=pltpu.HBM)
    vmem_spec = pl.BlockSpec(memory_space=pltpu.VMEM)
    return pl.pallas_call(
        functools.partial(kernel, sizes),
        out_shape=jax.ShapeDtypeStruct((pieces, width), bf),
        in_specs=[vmem_spec] + [hbm_spec] * 5,
        out_specs=vmem_spec,
        scratch_shapes=[
            pltpu.VMEM(routes.shape, routes.dtype),
            vmem(probs.shape),
            vmem((width, hidden)),
            vmem((width, hidden)),
            vmem((width, hidden)),
            vmem((2, ring, ranks, width)),
            vmem((ring, ranks, width)),
            vmem((ring, 2, ranks, width)),
            vmem((2, groups // 2, ring, ranks, width)),
            vmem((2, groups // 2, ring, 2, ranks, width)),
            vmem((ranks, chunk, width)),
            vmem((ranks, 2, chunk, width)),
            vmem((depth, chunk, width)),
            vmem((depth // 2, 2, chunk, width)),
            vmem((3, 2, ring, ranks * chunk, part)),
            vmem((3, 2, ring, ranks * chunk, part)),
            vmem((3, 2, ranks, chunk, part)),
            vmem((3, 2, ranks, chunk, part)),
            vmem((ranks, ring, chunk, part)),
            vmem((ranks, ring, chunk, part)),
            vmem((ring, chunk, part)),
            vmem((ring, chunk, part)),
            vmem((2, depth, 2, chunk, part)),
            vmem((depth, chunk, width)),
            vmem((depth, chunk, width)),
            vmem((groups, ring, ranks, width)),
            vmem((ring, groups, ranks, width)),
            dma((3,)),
            dma((2,)),
            dma(()),
            dma(()),
            dma((2, groups // 2, ring)),
            dma((2, groups // 2, ring)),
            dma((2,)),
            dma((2,)),
            dma((2, depth)),
            dma((2, depth)),
            dma((3, 2, ring)),
            dma((3, 2, ring)),
            dma((3, 2, ranks)),
            dma((3, 2, ranks)),
            dma((ranks,)),
            dma((ranks,)),
            dma((ring,)),
            dma((ring,)),
            dma((2, ranks)),
            dma((2, ranks)),
            dma((2, ranks, ring)),
            dma((2, ranks, ring)),
            dma((depth,)),
            dma((depth,)),
            dma((groups, ring)),
            dma((groups, ring)),
        ],
        compiler_params=pltpu.CompilerParams(
            collective_id=0, has_side_effects=True, vmem_limit_bytes=55168 * 1024
        ),
    )(tokens, routes, probs, w_gate, w_up, w_down)


def on_device(x_rows, grad_rows, routes, probs, w_gate, w_up, w_down, sizes):
    groups, blocks, ranks, ring, slots = sizes
    pieces, width = ranks * ring, w_gate.shape[1]
    tokens = jnp.stack([x_rows.reshape(pieces, width), grad_rows.reshape(pieces, width)])
    by_column = [jnp.swapaxes(array[:, :, 0], 1, 2) for array in (routes, probs)]
    result = run(sizes, tokens, *by_column, w_gate[0], w_up[0], jnp.swapaxes(w_down[0], 0, 1))
    return result.reshape(x_rows.shape)


def solution(mesh):
    sizes = (mesh.shape["group"], BLOCKS, RANKS, RING, SLOTS)
    in_specs = (
        P("group", "expert", None, None),
        P("group", "expert", None, None),
        P(),
        P(),
        P(("group", "expert"), None, None),
        P(("group", "expert"), None, None),
        P(("group", "expert"), None, None),
    )
    return jax.shard_map(
        functools.partial(on_device, sizes=sizes),
        mesh=mesh,
        in_specs=in_specs,
        out_specs=P("group", "expert", None, None),
        check_vma=False,
    )
```

```python
import functools

import jax
import jax.numpy as jnp
from jax import lax
from jax.experimental import pallas as pl
from jax.experimental.pallas import tpu as pltpu
from jax.sharding import PartitionSpec as P

MESH = pl.DeviceIdType.MESH
BLOCKS = 4
RANKS = 4
RING = 4
SLOTS = 4


def low(value, size):
    return value & (size - 1)


def high(value, size):
    return value >> (size.bit_length() - 1)


def onehot(mask):
    return jnp.where(mask, 1.0, 0.0).astype(jnp.bfloat16)


def exact_dot(left, right):
    return jnp.dot(left, right, preferred_element_type=jnp.float32)


def dot_nt(left, right):
    return lax.dot_general(left, right, (((1,), (1,)), ((), ())), preferred_element_type=jnp.float32)


def kernel(
    sizes,
    x_hbm,
    g_hbm,
    route_hbm,
    prob_hbm,
    wg_hbm,
    wu_hbm,
    wd_hbm,
    out_ref,
    route_ref,
    prob_ref,
    wg,
    wu,
    wd,
    raw,
    tok,
    landed,
    pair,
    got_a,
    got_b,
    blk,
    blk_b,
    rows,
    rows_b,
    part,
    got_rx,
    part_z,
    got_rz,
    part_zb,
    got_zb,
    part_xb,
    got_rxb,
    grads,
    ret,
    got_ret,
    scat,
    fin,
    w_sem,
    m_sem,
    t_sem,
    p_send,
    p_recv,
    a_send,
    a_recv,
    c_send,
    c_recv,
    z_send,
    z_recv,
    rx_send,
    rx_recv,
    rz_send,
    rz_recv,
    bz_send,
    bz_recv,
    bx_send,
    bx_recv,
    gz_send,
    gz_recv,
    gx_send,
    gx_recv,
    tz_send,
    tz_recv,
    tg_send,
    tg_recv,
):
    groups, blocks, ranks, ring, slots = sizes
    depth = blocks * ranks
    pieces = ranks * ring
    chunk = ring * slots
    lines = groups // 2
    half = depth // 2
    width = wg.shape[0]
    hidden = wg.shape[1] // 2
    my_g = lax.axis_index("group")
    my_e = lax.axis_index("expert")
    my_x = low(my_e, ring)
    my_z = high(my_e, ring)
    my_r = low(my_z, ranks)
    z_base = my_z - my_r
    my_core = low(my_g, 2)
    my_y = high(my_g, 2)
    my_half = high(my_z, half)

    def chunk_of(z):
        return low(z, half) * 2 + high(z, half)

    def z_of(at):
        return low(at, 2) * half + high(at, 2)

    def at_x(x):
        return (my_g, my_z * ring + x)

    def at_z(z):
        return (my_g, z * ring + my_x)

    def at_g(g):
        return (g, my_e)

    def at_gx(g, x):
        return (g, my_z * ring + x)

    def remote(src, dst, send, recv, device):
        return pltpu.make_async_remote_copy(
            src_ref=src, dst_ref=dst, send_sem=send, recv_sem=recv, device_id=device, device_id_type=MESH
        )

    around = sorted(range(1, ring), key=lambda d: min(d, ring - d))
    sent = []

    def go(copy):
        copy.start()
        sent.append(copy)

    token_copies = [
        pltpu.make_async_copy(source, raw.at[at], t_sem.at[at]) for at, source in enumerate((x_hbm, g_hbm))
    ]
    for copy in token_copies:
        copy.start()
    map_copies = [
        pltpu.make_async_copy(source, target, m_sem.at[at])
        for at, (source, target) in enumerate(((route_hbm, route_ref), (prob_hbm, prob_ref)))
    ]
    for copy in map_copies:
        copy.start()
    weight_copies = [
        pltpu.make_async_copy(source, target, w_sem.at[at])
        for at, (source, target) in enumerate(((wg_hbm, wg), (wu_hbm, wu), (wd_hbm, wd)))
    ]
    for copy in weight_copies:
        copy.start()

    barrier = pltpu.get_barrier_semaphore()
    column = [(dg, dx) for dg in range(groups) for dx in range(ring) if dg or dx]
    for dg, dx in column:
        device = at_gx(low(my_g + dg, groups), low(my_x + dx, ring))
        pl.semaphore_signal(barrier, inc=1, device_id=device, device_id_type=MESH)
    for d in range(1, depth):
        pl.semaphore_signal(barrier, inc=1, device_id=at_z(low(my_z + d, depth)), device_id_type=MESH)

    for a in range(2):
        token_copies[a].wait()
        line = raw[a].astype(jnp.float32)
        order = [r * ring + x for x in range(ring) for r in range(ranks)]
        cut = jnp.concatenate([line[:, p * width : (p + 1) * width] for p in order], axis=0)
        tok[a] = cut.astype(jnp.bfloat16).reshape(ring, ranks, width)
    pl.semaphore_wait(barrier, groups * ring - 1 + depth - 1)

    steps = [(dy, dx) for dy in range(lines) for dx in range(ring) if dy or dx]
    steps.sort(key=lambda step: -min(step[0], lines - step[0]) - min(step[1], ring - step[1]))

    def spread(a, source, target):
        for dy, dx in steps:
            y, x = low(my_y + dy, lines), low(my_x + dx, ring)
            device = at_gx(y * 2 + my_core, x)
            go(remote(source.at[x], target.at[my_core, my_y, my_x], a_send.at[a, dy, dx], a_recv.at[a, dy, dx], device))
        target[my_core, my_y, my_x] = source[my_x]

    def share(a, target):
        for dy, dx in steps:
            slot = target.at[my_core, low(my_y - dy, lines), low(my_x - dx, ring)]
            remote(slot, slot, a_send.at[a, dy, dx], a_recv.at[a, dy, dx], at_g(my_g)).wait_recv()
        mine = target.at[my_core]
        go(remote(mine, mine, c_send.at[a], c_recv.at[a], at_g(my_y * 2 + 1 - my_core)))

    def wait_share(a, target):
        slot = target.at[1 - my_core]
        remote(slot, slot, c_send.at[a], c_recv.at[a], at_g(my_g)).wait_recv()

    spread(0, tok.at[0], got_a)
    go(remote(tok.at[1], landed, p_send, p_recv, at_z(low(my_z + half, depth))))
    slot_rows = ring * ranks * slots
    token_rows = groups * pieces

    for copy in map_copies:
        copy.wait()
    route = route_ref[...]
    columns = route.shape[2]
    in_group = jnp.max(jnp.where(high(route, blocks) == my_g, 1.0, 0.0), axis=1)
    expert = my_g * blocks + high(my_z, ranks)
    weight = jnp.sum(jnp.where(route == expert, prob_ref[...].astype(jnp.float32), 0.0), axis=1)
    count = jnp.zeros((1, columns), jnp.float32)
    slot_token = [count] * slots
    slot_weight = [count] * slots
    for m in range(groups):
        named = in_group[m : m + 1]
        for s in range(slots):
            here = jnp.where(count == s, named, 0.0)
            slot_token[s] += here * (m % 2 * lines + m // 2)
            slot_weight[s] += here * weight[m : m + 1]
        count += named
    row = lax.broadcasted_iota(jnp.int32, (chunk, columns), 0)
    owned = z_of(my_x * ranks + my_r) * ring
    row_p = jnp.zeros((chunk, columns), jnp.float32)
    for s in range(slots):
        row_p = jnp.where(low(row, slots) == s, slot_weight[s], row_p)
    owner = owned + high(row, slots) == lax.broadcasted_iota(jnp.int32, (chunk, columns), 1)
    row_p = jnp.sum(jnp.where(owner, row_p, 0.0), axis=1, keepdims=True)

    def picking(z):
        row = lax.broadcasted_iota(jnp.int32, (slot_rows, columns), 0)
        token = jnp.zeros((slot_rows, columns), jnp.float32)
        for s in range(slots):
            token = jnp.where(low(row, slots) == s, slot_token[s], token)
        at = z * ring + low(high(row, slots), ring)
        token = jnp.where(lax.broadcasted_iota(jnp.int32, (slot_rows, columns), 1) == at, token, 0.0)
        token = jnp.sum(token, axis=1, keepdims=True).astype(jnp.int32)
        row = lax.broadcasted_iota(jnp.int32, (slot_rows, 1), 0)
        rest = high(row, slots)
        wanted = (token * ring + low(rest, ring)) * ranks + high(rest, ring)
        return onehot(wanted == lax.broadcasted_iota(jnp.int32, (slot_rows, token_rows), 1))

    pick = picking(my_z)
    pick_pair = [picking(h * half + low(my_z, half)) for h in range(2)]

    near = list(range(1, depth // 4 + 1)) + list(range(depth - depth // 4 + 1, depth))
    near.sort(key=lambda d: min(d, depth - d))
    all_z = sorted(range(1, depth), key=lambda d: min(d, depth - d))

    way = 1 - 2 * my_core

    def send_deep(a, steps, source, slot):
        for d in steps:
            to = low(my_z + way * d, depth)
            go(remote(source.at[low(to, ranks)], slot, z_send.at[a, d], z_recv.at[a, d], at_z(to)))
        slot[...] = source[my_r]

    def wait_deep(a, steps, slot_from):
        for d in steps:
            slot = slot_from(low(my_z - way * d, depth))
            remote(slot, slot, z_send.at[a, d], z_recv.at[a, d], at_z(my_z)).wait_recv()

    def half_of(weight, h):
        return weight[:, h * hidden : (h + 1) * hidden]

    def ring_send(q, h, value):
        part[q, h] = value.astype(jnp.bfloat16).reshape(ring, ranks * chunk, hidden)
        for d in around:
            to = low(my_x + d, ring)
            go(remote(part.at[q, h, to], got_rx.at[q, h, d], rx_send.at[q, h, d], rx_recv.at[q, h, d], at_x(to)))

    def line_send(q, h):
        total = part[q, h, my_x].astype(jnp.float32)
        for d in around:
            slot = got_rx.at[q, h, d]
            remote(slot, slot, rx_send.at[q, h, d], rx_recv.at[q, h, d], at_x(my_x)).wait_recv()
            total += got_rx[q, h, d].astype(jnp.float32)
        part_z[q, h] = total.astype(jnp.bfloat16).reshape(ranks, chunk, hidden)
        for d in range(1, ranks):
            to = my_r ^ d
            device = at_z(z_base + to)
            go(remote(part_z.at[q, h, to], got_rz.at[q, h, d], rz_send.at[q, h, d], rz_recv.at[q, h, d], device))

    def line_sum(q, h):
        total = part_z[q, h, my_r].astype(jnp.float32)
        for d in range(1, ranks):
            slot = got_rz.at[q, h, d]
            remote(slot, slot, rz_send.at[q, h, d], rz_recv.at[q, h, d], at_z(my_z)).wait_recv()
            total += got_rz[q, h, d].astype(jnp.float32)
        return total

    mine = my_x * ranks + my_r

    def activate(h, back):
        gate = line_sum(0, h)
        up = line_sum(1, h)
        back = back() * row_p
        sig = 1.0 / (1.0 + jnp.exp(-gate))
        grads[h, mine, 0] = (back * up * sig * (1.0 + gate * (1.0 - sig))).astype(jnp.bfloat16)
        grads[h, mine, 1] = (back * gate * sig).astype(jnp.bfloat16)
        held = grads.at[h, mine]
        for j in range(1, ranks):
            go(remote(held, held, gz_send.at[h, j], gz_recv.at[h, j], at_z(z_base + (my_r ^ j))))
        pass_on(h, 0)

    def pass_on(h, j):
        held = grads.at[h, my_x * ranks + (my_r ^ j)]
        if j:
            remote(held, held, gz_send.at[h, j], gz_recv.at[h, j], at_z(my_z)).wait_recv()
        for d in around:
            go(remote(held, held, gx_send.at[h, j, d], gx_recv.at[h, j, d], at_x(low(my_x + d, ring))))

    share(0, got_a)
    remote(landed, landed, p_send, p_recv, at_z(my_z)).wait_recv()
    pair[:, my_half] = tok[1]
    pair[:, 1 - my_half] = landed[...]
    spread(1, pair, got_b)
    wait_share(0, got_a)
    chosen = exact_dot(pick, got_a[...].reshape(token_rows, width)).astype(jnp.bfloat16)
    blk[...] = chosen.reshape(ranks, chunk, width)
    send_deep(0, all_z, blk, rows.at[chunk_of(my_z)])
    share(1, got_b)
    wait_share(1, got_b)
    for h in range(2):
        chosen = exact_dot(pick_pair[h], got_b[:, :, :, h].reshape(token_rows, width)).astype(jnp.bfloat16)
        blk_b[:, h] = chosen.reshape(ranks, chunk, width)
    send_deep(1, near, blk_b, rows_b.at[low(my_z, half)])
    wait_deep(0, all_z, lambda z: rows.at[chunk_of(z)])
    rows_x = rows[...].reshape(depth * chunk, width)
    weight_copies[0].wait()
    weight_copies[1].wait()
    for h in range(2):
        ring_send(0, h, exact_dot(rows_x, half_of(wg, h)))
        ring_send(1, h, exact_dot(rows_x, half_of(wu, h)))
    wait_deep(1, near, lambda z: rows_b.at[low(z, half)])
    weight_copies[2].wait()
    rows_g = rows_b[...].reshape(depth * chunk, width)
    back_part = exact_dot(rows_g, half_of(wd, 0)).astype(jnp.bfloat16).reshape(ring, ranks, chunk, hidden)
    for r in range(ranks):
        part_zb[r] = back_part[:, r]
    for d in range(1, ranks):
        to = my_r ^ d
        go(remote(part_zb.at[to], got_zb.at[d], bz_send.at[d], bz_recv.at[d], at_z(z_base + to)))
    ring_send(2, 1, exact_dot(rows_g, half_of(wd, 1)))
    line_send(0, 0)
    line_send(1, 0)
    total = part_zb[my_r].astype(jnp.float32)
    for d in range(1, ranks):
        slot = got_zb.at[d]
        remote(slot, slot, bz_send.at[d], bz_recv.at[d], at_z(my_z)).wait_recv()
        total += got_zb[d].astype(jnp.float32)
    part_xb[...] = total.astype(jnp.bfloat16)
    for d in around:
        to = low(my_x + d, ring)
        go(remote(part_xb.at[to], got_rxb.at[d], bx_send.at[d], bx_recv.at[d], at_x(to)))
    line_send(0, 1)
    line_send(1, 1)
    line_send(2, 1)

    def back_first():
        back = part_xb[my_x].astype(jnp.float32)
        for d in around:
            slot = got_rxb.at[d]
            remote(slot, slot, bx_send.at[d], bx_recv.at[d], at_x(my_x)).wait_recv()
            back += got_rxb[d].astype(jnp.float32)
        return back

    activate(0, back_first)
    activate(1, lambda: line_sum(2, 1))
    for h in range(2):
        for j in range(1, ranks):
            pass_on(h, j)

    for d in [0] + around:
        owner = low(my_x - d, ring)
        first = owner * ranks
        if d:
            for h in range(2):
                for j in range(ranks):
                    slot = grads.at[h, first + (my_r ^ j)]
                    remote(slot, slot, gx_send.at[h, j, d], gx_recv.at[h, j, d], at_x(my_x)).wait_recv()
        result = jnp.zeros((ranks * chunk, width), jnp.float32)
        for h in range(2):
            both = grads[h, pl.ds(first, ranks)]
            for q, weight in enumerate((wg, wu)):
                result += dot_nt(both[:, q].reshape(ranks * chunk, hidden), half_of(weight, h))
        ret[pl.ds(first, ranks)] = result.astype(jnp.bfloat16).reshape(ranks, chunk, width)
        for j in range(ranks):
            at = first + j
            to = z_of(at)

            @pl.when(to != my_z)
            def _(at=at, to=to):
                remote(ret.at[at], got_ret.at[my_z], tz_send.at[to], tz_recv.at[my_z], at_z(to)).start()

    got_ret[my_z] = ret[chunk_of(my_z)]
    for d in range(1, depth):
        source = low(my_z - d, depth)
        slot = got_ret.at[source]
        remote(slot, slot, tz_send.at[source], tz_recv.at[source], at_z(my_z)).wait_recv()
    folded = got_ret[:ranks].astype(jnp.float32)
    for block in range(1, blocks):
        folded += got_ret[block * ranks : (block + 1) * ranks].astype(jnp.float32)
    folded = folded.astype(jnp.bfloat16).reshape(slot_rows, width)
    scattered = lax.dot_general(pick, folded, (((0,), (0,)), ((), ())), preferred_element_type=jnp.float32)
    scat[...] = scattered.astype(jnp.bfloat16).reshape(groups, ring, ranks, width)

    def place(g):
        return low(g, 2) * lines + high(g, 2)

    def hops(step):
        dy = step[0] // 2
        return min(dy, lines - dy) + min(step[1], ring - step[1])

    column.sort(key=lambda step: -hops(step))
    for dg, dx in column:
        g, x = low(my_g + dg, groups), low(my_x + dx, ring)
        go(remote(scat.at[place(g), x], fin.at[my_x, dg], tg_send.at[dg, dx], tg_recv.at[dg, dx], at_gx(g, x)))
    fin[my_x, 0] = scat[place(my_g), my_x]
    shape = (pieces, token_rows)
    row = lax.broadcasted_iota(jnp.int32, shape, 0)
    col = lax.broadcasted_iota(jnp.int32, shape, 1)
    same_x = high(high(col, ranks), groups) == low(row, ring)
    gather = onehot(same_x & (low(col, ranks) == high(row, ring)))
    for dg, dx in column:
        slot = fin.at[low(my_x - dx, ring), dg]
        remote(slot, slot, tg_send.at[dg, dx], tg_recv.at[dg, dx], at_g(my_g)).wait_recv()
    out_ref[...] = exact_dot(gather, fin[...].reshape(token_rows, width)).astype(jnp.bfloat16)

    for copy in sent:
        copy.wait_send()
    for d in range(1, depth):
        to = low(my_z + d, depth)
        remote(ret.at[chunk_of(to)], got_ret.at[my_z], tz_send.at[to], tz_recv.at[my_z], at_z(to)).wait_send()


def run(sizes, x_row, grad_row, routes, probs, w_gate, w_up, w_down):
    groups, blocks, ranks, ring, slots = sizes
    depth, pieces, chunk = blocks * ranks, ranks * ring, ring * slots
    width, hidden = w_gate.shape
    part = hidden // 2
    bf = jnp.bfloat16
    vmem = functools.partial(pltpu.VMEM, dtype=bf)
    dma = pltpu.SemaphoreType.DMA
    hbm_spec = pl.BlockSpec(memory_space=pltpu.HBM)
    return pl.pallas_call(
        functools.partial(kernel, sizes),
        out_shape=jax.ShapeDtypeStruct((pieces, width), bf),
        in_specs=[hbm_spec] * 7,
        out_specs=pl.BlockSpec(memory_space=pltpu.VMEM),
        scratch_shapes=[
            pltpu.VMEM(routes.shape, routes.dtype),
            vmem(probs.shape),
            vmem((width, hidden)),
            vmem((width, hidden)),
            vmem((width, hidden)),
            vmem((2,) + x_row.shape),
            vmem((2, ring, ranks, width)),
            vmem((ring, ranks, width)),
            vmem((ring, 2, ranks, width)),
            vmem((2, groups // 2, ring, ranks, width)),
            vmem((2, groups // 2, ring, 2, ranks, width)),
            vmem((ranks, chunk, width)),
            vmem((ranks, 2, chunk, width)),
            vmem((depth, chunk, width)),
            vmem((depth // 2, 2, chunk, width)),
            vmem((3, 2, ring, ranks * chunk, part)),
            vmem((3, 2, ring, ranks * chunk, part)),
            vmem((3, 2, ranks, chunk, part)),
            vmem((3, 2, ranks, chunk, part)),
            vmem((ranks, ring, chunk, part)),
            vmem((ranks, ring, chunk, part)),
            vmem((ring, chunk, part)),
            vmem((ring, chunk, part)),
            vmem((2, depth, 2, chunk, part)),
            vmem((depth, chunk, width)),
            vmem((depth, chunk, width)),
            vmem((groups, ring, ranks, width)),
            vmem((ring, groups, ranks, width)),
            dma((3,)),
            dma((2,)),
            dma((2,)),
            dma(()),
            dma(()),
            dma((2, groups // 2, ring)),
            dma((2, groups // 2, ring)),
            dma((2,)),
            dma((2,)),
            dma((2, depth)),
            dma((2, depth)),
            dma((3, 2, ring)),
            dma((3, 2, ring)),
            dma((3, 2, ranks)),
            dma((3, 2, ranks)),
            dma((ranks,)),
            dma((ranks,)),
            dma((ring,)),
            dma((ring,)),
            dma((2, ranks)),
            dma((2, ranks)),
            dma((2, ranks, ring)),
            dma((2, ranks, ring)),
            dma((depth,)),
            dma((depth,)),
            dma((groups, ring)),
            dma((groups, ring)),
        ],
        compiler_params=pltpu.CompilerParams(
            collective_id=0, has_side_effects=True, vmem_limit_bytes=55216 * 1024
        ),
    )(x_row, grad_row, routes, probs, w_gate, w_up, w_down)


def on_device(x_rows, grad_rows, routes, probs, w_gate, w_up, w_down, sizes):
    rows = [array.reshape(1, -1) for array in (x_rows, grad_rows)]
    by_column = [jnp.swapaxes(array[:, :, 0], 1, 2) for array in (routes, probs)]
    result = run(sizes, *rows, *by_column, w_gate[0], w_up[0], jnp.swapaxes(w_down[0], 0, 1))
    return result.reshape(x_rows.shape)


def solution(mesh):
    sizes = (mesh.shape["group"], BLOCKS, RANKS, RING, SLOTS)
    in_specs = (
        P("group", "expert", None, None),
        P("group", "expert", None, None),
        P(),
        P(),
        P(("group", "expert"), None, None),
        P(("group", "expert"), None, None),
        P(("group", "expert"), None, None),
    )
    return jax.shard_map(
        functools.partial(on_device, sizes=sizes),
        mesh=mesh,
        in_specs=in_specs,
        out_specs=P("group", "expert", None, None),
        check_vma=False,
    )
```

```python
import functools

import jax
import jax.numpy as jnp
from jax import lax
from jax.experimental import pallas as pl
from jax.experimental.pallas import tpu as pltpu
from jax.sharding import PartitionSpec as P

MESH = pl.DeviceIdType.MESH
BLOCKS = 4
RANKS = 4
RING = 4
SLOTS = 4


def low(value, size):
    return value & (size - 1)


def high(value, size):
    return value >> (size.bit_length() - 1)


def onehot(mask):
    return jnp.where(mask, 1.0, 0.0).astype(jnp.bfloat16)


def exact_dot(left, right):
    return jnp.dot(left, right, preferred_element_type=jnp.float32)


def dot_nt(left, right):
    return lax.dot_general(left, right, (((1,), (1,)), ((), ())), preferred_element_type=jnp.float32)


def kernel(
    sizes,
    x_hbm,
    g_hbm,
    route_hbm,
    prob_hbm,
    wg_hbm,
    wu_hbm,
    wd_hbm,
    out_ref,
    route_ref,
    prob_ref,
    wg,
    wu,
    wd,
    raw,
    tok,
    landed,
    pair,
    got_a,
    got_b,
    blk,
    blk_b,
    rows,
    rows_b,
    part,
    got_rx,
    mid,
    part_z,
    got_rz,
    part_zb,
    got_zb,
    part_xb,
    got_rxb,
    grads,
    ret,
    got_ret,
    scat,
    fin,
    w_sem,
    m_sem,
    t_sem,
    p_send,
    p_recv,
    a_send,
    a_recv,
    c_send,
    c_recv,
    z_send,
    z_recv,
    rx_send,
    rx_recv,
    m_send,
    m_recv,
    rz_send,
    rz_recv,
    bz_send,
    bz_recv,
    bx_send,
    bx_recv,
    gz_send,
    gz_recv,
    gx_send,
    gx_recv,
    tz_send,
    tz_recv,
    tg_send,
    tg_recv,
):
    groups, blocks, ranks, ring, slots = sizes
    depth = blocks * ranks
    pieces = ranks * ring
    chunk = ring * slots
    lines = groups // 2
    half = depth // 2
    width = wg.shape[0]
    hidden = wg.shape[1] // 2
    my_g = lax.axis_index("group")
    my_e = lax.axis_index("expert")
    my_x = low(my_e, ring)
    my_z = high(my_e, ring)
    my_r = low(my_z, ranks)
    z_base = my_z - my_r
    my_core = low(my_g, 2)
    my_y = high(my_g, 2)
    my_half = high(my_z, half)

    def chunk_of(z):
        return low(z, half) * 2 + high(z, half)

    def z_of(at):
        return low(at, 2) * half + high(at, 2)

    def at_x(x):
        return (my_g, my_z * ring + x)

    def at_z(z):
        return (my_g, z * ring + my_x)

    def at_g(g):
        return (g, my_e)

    def at_gx(g, x):
        return (g, my_z * ring + x)

    def remote(src, dst, send, recv, device):
        return pltpu.make_async_remote_copy(
            src_ref=src, dst_ref=dst, send_sem=send, recv_sem=recv, device_id=device, device_id_type=MESH
        )

    around = sorted(range(1, ring), key=lambda d: min(d, ring - d))
    sent = []

    def go(copy):
        copy.start()
        sent.append(copy)

    token_copies = [
        pltpu.make_async_copy(source, raw.at[at], t_sem.at[at]) for at, source in enumerate((x_hbm, g_hbm))
    ]
    for copy in token_copies:
        copy.start()
    map_copies = [
        pltpu.make_async_copy(source, target, m_sem.at[at])
        for at, (source, target) in enumerate(((route_hbm, route_ref), (prob_hbm, prob_ref)))
    ]
    for copy in map_copies:
        copy.start()
    weight_copies = [
        pltpu.make_async_copy(source, target, w_sem.at[at])
        for at, (source, target) in enumerate(((wg_hbm, wg), (wu_hbm, wu), (wd_hbm, wd)))
    ]
    for copy in weight_copies:
        copy.start()

    barrier = pltpu.get_barrier_semaphore()
    column = [(dg, dx) for dg in range(groups) for dx in range(ring) if dg or dx]
    for dg, dx in column:
        device = at_gx(low(my_g + dg, groups), low(my_x + dx, ring))
        pl.semaphore_signal(barrier, inc=1, device_id=device, device_id_type=MESH)
    for d in range(1, depth):
        pl.semaphore_signal(barrier, inc=1, device_id=at_z(low(my_z + d, depth)), device_id_type=MESH)

    for a in range(2):
        token_copies[a].wait()
        line = raw[a].astype(jnp.float32)
        order = [r * ring + x for x in range(ring) for r in range(ranks)]
        cut = jnp.concatenate([line[:, p * width : (p + 1) * width] for p in order], axis=0)
        tok[a] = cut.astype(jnp.bfloat16).reshape(ring, ranks, width)
    pl.semaphore_wait(barrier, groups * ring - 1 + depth - 1)

    steps = [(dy, dx) for dy in range(lines) for dx in range(ring) if dy or dx]
    steps.sort(key=lambda step: -min(step[0], lines - step[0]) - min(step[1], ring - step[1]))

    def spread(a, source, target):
        for dy, dx in steps:
            y, x = low(my_y + dy, lines), low(my_x + dx, ring)
            device = at_gx(y * 2 + my_core, x)
            go(remote(source.at[x], target.at[my_core, my_y, my_x], a_send.at[a, dy, dx], a_recv.at[a, dy, dx], device))
        target[my_core, my_y, my_x] = source[my_x]

    def share(a, target):
        for dy, dx in steps:
            slot = target.at[my_core, low(my_y - dy, lines), low(my_x - dx, ring)]
            remote(slot, slot, a_send.at[a, dy, dx], a_recv.at[a, dy, dx], at_g(my_g)).wait_recv()
        mine = target.at[my_core]
        go(remote(mine, mine, c_send.at[a], c_recv.at[a], at_g(my_y * 2 + 1 - my_core)))

    def wait_share(a, target):
        slot = target.at[1 - my_core]
        remote(slot, slot, c_send.at[a], c_recv.at[a], at_g(my_g)).wait_recv()

    spread(0, tok.at[0], got_a)
    go(remote(tok.at[1], landed, p_send, p_recv, at_z(low(my_z + half, depth))))
    slot_rows = ring * ranks * slots
    token_rows = groups * pieces

    for copy in map_copies:
        copy.wait()
    route = route_ref[...]
    columns = route.shape[2]
    in_group = jnp.max(jnp.where(high(route, blocks) == my_g, 1.0, 0.0), axis=1)
    expert = my_g * blocks + high(my_z, ranks)
    weight = jnp.sum(jnp.where(route == expert, prob_ref[...].astype(jnp.float32), 0.0), axis=1)
    count = jnp.zeros((1, columns), jnp.float32)
    slot_token = [count] * slots
    slot_weight = [count] * slots
    for m in range(groups):
        named = in_group[m : m + 1]
        for s in range(slots):
            here = jnp.where(count == s, named, 0.0)
            slot_token[s] += here * (m % 2 * lines + m // 2)
            slot_weight[s] += here * weight[m : m + 1]
        count += named
    row = lax.broadcasted_iota(jnp.int32, (chunk, columns), 0)
    owned = z_of(my_x * ranks + my_r) * ring
    row_p = jnp.zeros((chunk, columns), jnp.float32)
    for s in range(slots):
        row_p = jnp.where(low(row, slots) == s, slot_weight[s], row_p)
    owner = owned + high(row, slots) == lax.broadcasted_iota(jnp.int32, (chunk, columns), 1)
    row_p = jnp.sum(jnp.where(owner, row_p, 0.0), axis=1, keepdims=True)

    def picking(z):
        row = lax.broadcasted_iota(jnp.int32, (slot_rows, columns), 0)
        token = jnp.zeros((slot_rows, columns), jnp.float32)
        for s in range(slots):
            token = jnp.where(low(row, slots) == s, slot_token[s], token)
        at = z * ring + low(high(row, slots), ring)
        token = jnp.where(lax.broadcasted_iota(jnp.int32, (slot_rows, columns), 1) == at, token, 0.0)
        token = jnp.sum(token, axis=1, keepdims=True).astype(jnp.int32)
        row = lax.broadcasted_iota(jnp.int32, (slot_rows, 1), 0)
        rest = high(row, slots)
        wanted = (token * ring + low(rest, ring)) * ranks + high(rest, ring)
        return onehot(wanted == lax.broadcasted_iota(jnp.int32, (slot_rows, token_rows), 1))

    pick = picking(my_z)
    pick_pair = [picking(h * half + low(my_z, half)) for h in range(2)]

    near = list(range(1, depth // 4 + 1)) + list(range(depth - depth // 4 + 1, depth))
    near.sort(key=lambda d: min(d, depth - d))
    all_z = sorted(range(1, depth), key=lambda d: min(d, depth - d))

    way = 1 - 2 * my_core

    def send_deep(a, steps, source, slot):
        for d in steps:
            to = low(my_z + way * d, depth)
            go(remote(source.at[low(to, ranks)], slot, z_send.at[a, d], z_recv.at[a, d], at_z(to)))
        slot[...] = source[my_r]

    def wait_deep(a, steps, slot_from):
        for d in steps:
            slot = slot_from(low(my_z - way * d, depth))
            remote(slot, slot, z_send.at[a, d], z_recv.at[a, d], at_z(my_z)).wait_recv()

    def half_of(weight, h):
        return weight[:, h * hidden : (h + 1) * hidden]

    def ring_send(q, h, value):
        part[q, h] = value.astype(jnp.bfloat16).reshape(ring, ranks * chunk, hidden)
        for d in around:
            to = low(my_x + d, ring)
            go(remote(part.at[q, h, to], got_rx.at[q, h, d], rx_send.at[q, h, d], rx_recv.at[q, h, d], at_x(to)))

    upper, lower = pl.ds(0, ranks * chunk // 2), pl.ds(ranks * chunk // 2, ranks * chunk // 2)
    right, left, across = low(my_x + 1, ring), low(my_x - 1, ring), low(my_x + 2, ring)
    legs = ((right, upper, lower), (left, lower, upper))

    def relay_send(q, h, value):
        part[q, h] = value.astype(jnp.bfloat16).reshape(ring, ranks * chunk, hidden)
        for at, (to, passed, direct) in enumerate(legs):
            source = part.at[q, h, across, passed]
            go(remote(source, mid.at[q, h, at], m_send.at[q, h, at], m_recv.at[q, h, at], at_x(to)))
        for at, (to, passed, direct) in enumerate(legs):
            source, target = part.at[q, h, to, direct], got_rx.at[q, h, at, direct]
            go(remote(source, target, rx_send.at[q, h, at], rx_recv.at[q, h, at], at_x(to)))

    def relay_pass(q, h):
        for at, (to, passed, direct) in enumerate(legs):
            slot = mid.at[q, h, at]
            remote(slot, slot, m_send.at[q, h, at], m_recv.at[q, h, at], at_x(my_x)).wait_recv()
            total = part[q, h, to, passed].astype(jnp.float32) + mid[q, h, at].astype(jnp.float32)
            part[q, h, to, passed] = total.astype(jnp.bfloat16)
            source, target = part.at[q, h, to, passed], got_rx.at[q, h, at, passed]
            go(remote(source, target, rx_send.at[q, h, 2 + at], rx_recv.at[q, h, 2 + at], at_x(to)))

    def relay_wait(q, h):
        for at, (to, passed, direct) in enumerate(legs):
            for sem, rows_at in ((at, direct), (2 + at, passed)):
                slot = got_rx.at[q, h, at, rows_at]
                remote(slot, slot, rx_send.at[q, h, sem], rx_recv.at[q, h, sem], at_x(my_x)).wait_recv()

    def line_send(q, h):
        total = part[q, h, my_x].astype(jnp.float32)
        if q < 2:
            relay_wait(q, h)
            total += got_rx[q, h, 0].astype(jnp.float32) + got_rx[q, h, 1].astype(jnp.float32)
        for d in around if q == 2 else ():
            slot = got_rx.at[q, h, d]
            remote(slot, slot, rx_send.at[q, h, d], rx_recv.at[q, h, d], at_x(my_x)).wait_recv()
            total += got_rx[q, h, d].astype(jnp.float32)
        part_z[q, h] = total.astype(jnp.bfloat16).reshape(ranks, chunk, hidden)
        for d in range(1, ranks):
            to = my_r ^ d
            device = at_z(z_base + to)
            go(remote(part_z.at[q, h, to], got_rz.at[q, h, d], rz_send.at[q, h, d], rz_recv.at[q, h, d], device))

    def line_sum(q, h):
        total = part_z[q, h, my_r].astype(jnp.float32)
        for d in range(1, ranks):
            slot = got_rz.at[q, h, d]
            remote(slot, slot, rz_send.at[q, h, d], rz_recv.at[q, h, d], at_z(my_z)).wait_recv()
            total += got_rz[q, h, d].astype(jnp.float32)
        return total

    mine = my_x * ranks + my_r

    def activate(h, back):
        gate = line_sum(0, h)
        up = line_sum(1, h)
        back = back() * row_p
        sig = 1.0 / (1.0 + jnp.exp(-gate))
        grads[h, mine, 0] = (back * up * sig * (1.0 + gate * (1.0 - sig))).astype(jnp.bfloat16)
        grads[h, mine, 1] = (back * gate * sig).astype(jnp.bfloat16)
        held = grads.at[h, mine]
        for j in range(1, ranks):
            go(remote(held, held, gz_send.at[h, j], gz_recv.at[h, j], at_z(z_base + (my_r ^ j))))
        pass_on(h, 0)

    def pass_on(h, j):
        held = grads.at[h, my_x * ranks + (my_r ^ j)]
        if j:
            remote(held, held, gz_send.at[h, j], gz_recv.at[h, j], at_z(my_z)).wait_recv()
        for d in around:
            go(remote(held, held, gx_send.at[h, j, d], gx_recv.at[h, j, d], at_x(low(my_x + d, ring))))

    share(0, got_a)
    remote(landed, landed, p_send, p_recv, at_z(my_z)).wait_recv()
    pair[:, my_half] = tok[1]
    pair[:, 1 - my_half] = landed[...]
    spread(1, pair, got_b)
    wait_share(0, got_a)
    chosen = exact_dot(pick, got_a[...].reshape(token_rows, width)).astype(jnp.bfloat16)
    blk[...] = chosen.reshape(ranks, chunk, width)
    send_deep(0, all_z, blk, rows.at[chunk_of(my_z)])
    share(1, got_b)
    wait_share(1, got_b)
    for h in range(2):
        chosen = exact_dot(pick_pair[h], got_b[:, :, :, h].reshape(token_rows, width)).astype(jnp.bfloat16)
        blk_b[:, h] = chosen.reshape(ranks, chunk, width)
    send_deep(1, near, blk_b, rows_b.at[low(my_z, half)])
    wait_deep(0, all_z, lambda z: rows.at[chunk_of(z)])
    rows_x = rows[...].reshape(depth * chunk, width)
    weight_copies[0].wait()
    weight_copies[1].wait()
    for h in range(2):
        relay_send(0, h, exact_dot(rows_x, half_of(wg, h)))
        relay_send(1, h, exact_dot(rows_x, half_of(wu, h)))
    wait_deep(1, near, lambda z: rows_b.at[low(z, half)])
    weight_copies[2].wait()
    rows_g = rows_b[...].reshape(depth * chunk, width)
    back_part = exact_dot(rows_g, half_of(wd, 0)).astype(jnp.bfloat16).reshape(ring, ranks, chunk, hidden)
    for r in range(ranks):
        part_zb[r] = back_part[:, r]
    for d in range(1, ranks):
        to = my_r ^ d
        go(remote(part_zb.at[to], got_zb.at[d], bz_send.at[d], bz_recv.at[d], at_z(z_base + to)))
    for h in range(2):
        for q in range(2):
            relay_pass(q, h)
    ring_send(2, 1, exact_dot(rows_g, half_of(wd, 1)))
    line_send(0, 0)
    line_send(1, 0)
    total = part_zb[my_r].astype(jnp.float32)
    for d in range(1, ranks):
        slot = got_zb.at[d]
        remote(slot, slot, bz_send.at[d], bz_recv.at[d], at_z(my_z)).wait_recv()
        total += got_zb[d].astype(jnp.float32)
    part_xb[...] = total.astype(jnp.bfloat16)
    for d in around:
        to = low(my_x + d, ring)
        go(remote(part_xb.at[to], got_rxb.at[d], bx_send.at[d], bx_recv.at[d], at_x(to)))
    line_send(0, 1)
    line_send(1, 1)
    line_send(2, 1)

    def back_first():
        back = part_xb[my_x].astype(jnp.float32)
        for d in around:
            slot = got_rxb.at[d]
            remote(slot, slot, bx_send.at[d], bx_recv.at[d], at_x(my_x)).wait_recv()
            back += got_rxb[d].astype(jnp.float32)
        return back

    activate(0, back_first)
    activate(1, lambda: line_sum(2, 1))
    for h in range(2):
        for j in range(1, ranks):
            pass_on(h, j)

    for d in [0] + around:
        owner = low(my_x - d, ring)
        first = owner * ranks
        if d:
            for h in range(2):
                for j in range(ranks):
                    slot = grads.at[h, first + (my_r ^ j)]
                    remote(slot, slot, gx_send.at[h, j, d], gx_recv.at[h, j, d], at_x(my_x)).wait_recv()
        result = jnp.zeros((ranks * chunk, width), jnp.float32)
        for h in range(2):
            both = grads[h, pl.ds(first, ranks)]
            for q, weight in enumerate((wg, wu)):
                result += dot_nt(both[:, q].reshape(ranks * chunk, hidden), half_of(weight, h))
        ret[pl.ds(first, ranks)] = result.astype(jnp.bfloat16).reshape(ranks, chunk, width)
        for j in range(ranks):
            at = first + j
            to = z_of(at)

            @pl.when(to != my_z)
            def _(at=at, to=to):
                remote(ret.at[at], got_ret.at[my_z], tz_send.at[to], tz_recv.at[my_z], at_z(to)).start()

    got_ret[my_z] = ret[chunk_of(my_z)]
    for d in range(1, depth):
        source = low(my_z - d, depth)
        slot = got_ret.at[source]
        remote(slot, slot, tz_send.at[source], tz_recv.at[source], at_z(my_z)).wait_recv()
    folded = got_ret[:ranks].astype(jnp.float32)
    for block in range(1, blocks):
        folded += got_ret[block * ranks : (block + 1) * ranks].astype(jnp.float32)
    folded = folded.astype(jnp.bfloat16).reshape(slot_rows, width)
    scattered = lax.dot_general(pick, folded, (((0,), (0,)), ((), ())), preferred_element_type=jnp.float32)
    scat[...] = scattered.astype(jnp.bfloat16).reshape(groups, ring, ranks, width)

    def place(g):
        return low(g, 2) * lines + high(g, 2)

    def hops(step):
        dy = step[0] // 2
        return min(dy, lines - dy) + min(step[1], ring - step[1])

    column.sort(key=lambda step: -hops(step))
    for dg, dx in column:
        g, x = low(my_g + dg, groups), low(my_x + dx, ring)
        go(remote(scat.at[place(g), x], fin.at[my_x, dg], tg_send.at[dg, dx], tg_recv.at[dg, dx], at_gx(g, x)))
    fin[my_x, 0] = scat[place(my_g), my_x]
    shape = (pieces, token_rows)
    row = lax.broadcasted_iota(jnp.int32, shape, 0)
    col = lax.broadcasted_iota(jnp.int32, shape, 1)
    same_x = high(high(col, ranks), groups) == low(row, ring)
    gather = onehot(same_x & (low(col, ranks) == high(row, ring)))
    for dg, dx in column:
        slot = fin.at[low(my_x - dx, ring), dg]
        remote(slot, slot, tg_send.at[dg, dx], tg_recv.at[dg, dx], at_g(my_g)).wait_recv()
    out_ref[...] = exact_dot(gather, fin[...].reshape(token_rows, width)).astype(jnp.bfloat16)

    for copy in sent:
        copy.wait_send()
    for d in range(1, depth):
        to = low(my_z + d, depth)
        remote(ret.at[chunk_of(to)], got_ret.at[my_z], tz_send.at[to], tz_recv.at[my_z], at_z(to)).wait_send()


def run(sizes, x_row, grad_row, routes, probs, w_gate, w_up, w_down):
    groups, blocks, ranks, ring, slots = sizes
    depth, pieces, chunk = blocks * ranks, ranks * ring, ring * slots
    width, hidden = w_gate.shape
    part = hidden // 2
    bf = jnp.bfloat16
    vmem = functools.partial(pltpu.VMEM, dtype=bf)
    dma = pltpu.SemaphoreType.DMA
    hbm_spec = pl.BlockSpec(memory_space=pltpu.HBM)
    return pl.pallas_call(
        functools.partial(kernel, sizes),
        out_shape=jax.ShapeDtypeStruct((pieces, width), bf),
        in_specs=[hbm_spec] * 7,
        out_specs=pl.BlockSpec(memory_space=pltpu.VMEM),
        scratch_shapes=[
            pltpu.VMEM(routes.shape, routes.dtype),
            vmem(probs.shape),
            vmem((width, hidden)),
            vmem((width, hidden)),
            vmem((width, hidden)),
            vmem((2,) + x_row.shape),
            vmem((2, ring, ranks, width)),
            vmem((ring, ranks, width)),
            vmem((ring, 2, ranks, width)),
            vmem((2, groups // 2, ring, ranks, width)),
            vmem((2, groups // 2, ring, 2, ranks, width)),
            vmem((ranks, chunk, width)),
            vmem((ranks, 2, chunk, width)),
            vmem((depth, chunk, width)),
            vmem((depth // 2, 2, chunk, width)),
            vmem((3, 2, ring, ranks * chunk, part)),
            vmem((3, 2, ring, ranks * chunk, part)),
            vmem((2, 2, 2, ranks * chunk // 2, part)),
            vmem((3, 2, ranks, chunk, part)),
            vmem((3, 2, ranks, chunk, part)),
            vmem((ranks, ring, chunk, part)),
            vmem((ranks, ring, chunk, part)),
            vmem((ring, chunk, part)),
            vmem((ring, chunk, part)),
            vmem((2, depth, 2, chunk, part)),
            vmem((depth, chunk, width)),
            vmem((depth, chunk, width)),
            vmem((groups, ring, ranks, width)),
            vmem((ring, groups, ranks, width)),
            dma((3,)),
            dma((2,)),
            dma((2,)),
            dma(()),
            dma(()),
            dma((2, groups // 2, ring)),
            dma((2, groups // 2, ring)),
            dma((2,)),
            dma((2,)),
            dma((2, depth)),
            dma((2, depth)),
            dma((3, 2, ring)),
            dma((3, 2, ring)),
            dma((2, 2, 2)),
            dma((2, 2, 2)),
            dma((3, 2, ranks)),
            dma((3, 2, ranks)),
            dma((ranks,)),
            dma((ranks,)),
            dma((ring,)),
            dma((ring,)),
            dma((2, ranks)),
            dma((2, ranks)),
            dma((2, ranks, ring)),
            dma((2, ranks, ring)),
            dma((depth,)),
            dma((depth,)),
            dma((groups, ring)),
            dma((groups, ring)),
        ],
        compiler_params=pltpu.CompilerParams(
            collective_id=0, has_side_effects=True, vmem_limit_bytes=55216 * 1024
        ),
    )(x_row, grad_row, routes, probs, w_gate, w_up, w_down)


def on_device(x_rows, grad_rows, routes, probs, w_gate, w_up, w_down, sizes):
    rows = [array.reshape(1, -1) for array in (x_rows, grad_rows)]
    by_column = [jnp.swapaxes(array[:, :, 0], 1, 2) for array in (routes, probs)]
    result = run(sizes, *rows, *by_column, w_gate[0], w_up[0], jnp.swapaxes(w_down[0], 0, 1))
    return result.reshape(x_rows.shape)


def solution(mesh):
    sizes = (mesh.shape["group"], BLOCKS, RANKS, RING, SLOTS)
    in_specs = (
        P("group", "expert", None, None),
        P("group", "expert", None, None),
        P(),
        P(),
        P(("group", "expert"), None, None),
        P(("group", "expert"), None, None),
        P(("group", "expert"), None, None),
    )
    return jax.shard_map(
        functools.partial(on_device, sizes=sizes),
        mesh=mesh,
        in_specs=in_specs,
        out_specs=P("group", "expert", None, None),
        check_vma=False,
    )
```
